512 devices in a mesh: lat: 32 (over z, y_lo), lon: 16 (over y_hi, x, core).
Axes of the slice: x: 4, y: 8 (y_hi: 2, y_lo: 4; y = y_hi * 4 + y_lo), z: 8, core: 2. Of those that a mesh axis runs over, the one named last changes fastest.
Arguments:
- state_field: bfloat16 [6, 384, 192, 192], P(None, 'lat', 'lon'), may hold values from -6 to 6
- attn_bias: bfloat16 [64, 6, 144, 144], P('lat'), may hold values from -8 to 300
- region_ids: int32 [384, 192], P('lat', 'lon'), may hold values from 0 to 3
- w_qkv: bfloat16 [192, 576], replicated, may hold values from -0.4375 to 0.4375
- w_out: bfloat16 [192, 192], replicated, may hold values from -0.4375 to 0.4375
- w_up: bfloat16 [192, 768], replicated, may hold values from -0.4375 to 0.4375
- w_down: bfloat16 [768, 192], replicated, may hold values from -0.21875 to 0.21875
Outputs:
- output: bfloat16 [6, 384, 192, 192], P(None, 'lat', 'lon')
The draws below stay inside these ranges and needn't reach their ends.
All inputs are finite; a program needn't handle non-finite values.
Results may differ from the reference program's by a relative error of at most 0.012.
Values may be sent and summed in bfloat16 or wider, within the bound.
A program may use at most 64 MiB of HBM per device.

```python
import jax
import jax.numpy as jnp
from jax import lax

C = 192
HEADS = 6
FF = 768
WZ = 2
WY = 6
WX = 12
WIN = 144
NLEV = 6
NLAT = 384
NLON = 192
NWLAT = 64


def draw_attn_bias(key, part):
    key = jax.random.fold_in(key, 7)
    shape = (NWLAT, HEADS, WIN, WIN)
    base = jnp.clip(jax.random.normal(key, shape, jnp.float32), -6.0, 6.0)
    return base.astype(jnp.bfloat16)


def plant(entries, key, smallest, top_value):
    index_at = [jax.random.randint(jax.random.fold_in(key, axis), (), 0, length) for axis, length in enumerate(entries.shape)]
    widest = entries.shape.index(max(entries.shape))
    next_to = index_at[:widest] + [(index_at[widest] + 1) % entries.shape[widest]] + index_at[widest + 1:]
    return entries.at[tuple(index_at)].set(smallest).at[tuple(next_to)].set(top_value)


def level_of(stream_key, shape, pieces, smallest, largest):
    factor_of, own = 1.0, jax.random.fold_in(stream_key, 6)
    for axis_at, parts in pieces:
        steps = jnp.exp(jax.random.uniform(jax.random.fold_in(own, axis_at), (parts,), jnp.float32, smallest / len(pieces), largest / len(pieces)))
        factor_of = factor_of * jnp.repeat(steps, shape[axis_at] // parts).reshape([-1 if axis == axis_at else 1 for axis in range(len(shape))])
    return factor_of


def normal_values(own_key, dims, scale, most, split=(), kind=jnp.bfloat16):
    entries = scale * jax.random.normal(own_key, dims, jnp.float32)
    if split:
        entries = entries * level_of(own_key, dims, split, -0.22, 0.18)
    return jnp.clip(entries, -most, most).astype(kind)


def setup_inputs(seed: int = 0) -> dict:
    seeds = jax.random.split(jax.random.key(seed), 8)
    return {
        "state_field": normal_values(seeds[0], (NLEV, NLAT, NLON, C), 1.0, 6.0, ((1, 32), (2, 16))),
        "attn_bias": draw_attn_bias(jax.random.fold_in(seeds[7], 71), 0),
        "region_ids": plant(jax.random.randint(seeds[2], (NLAT, NLON), 0, 4), jax.random.fold_in(seeds[2], 1), 0, 3).astype(jnp.int32),
        "w_qkv": normal_values(seeds[3], (C, 3 * C), C ** -0.5, 0.4375),
        "w_out": normal_values(seeds[4], (C, C), C ** -0.5, 0.4375),
        "w_up": normal_values(seeds[5], (C, FF), C ** -0.5, 0.4375),
        "w_down": normal_values(seeds[6], (FF, C), FF ** -0.5, 0.21875),
    }


epsilon = 1e-05

def layer_norm(values):
    average = lax.optimization_barrier(jnp.mean(values, axis=-1, keepdims=True))
    centred = values - average
    variance = lax.optimization_barrier(jnp.mean(centred * centred, axis=-1, keepdims=True))
    return centred * lax.rsqrt(variance + epsilon)

def reference(state_field, attn_bias, region_ids, w_qkv, w_out, w_up, w_down):
    lat_half = WY // 2
    lon_half = WX // 2
    lev_blocks = NLEV // WZ
    lat_blocks = NLAT // WY
    lon_blocks = NLON // WX
    head_dim = C // HEADS
    normed = layer_norm(state_field.astype(jnp.float32)).astype(jnp.bfloat16)
    rolled = jnp.roll(normed, -(WZ // 2), axis=0)
    rolled = jnp.concatenate([rolled[:, lat_half:], jnp.zeros((NLEV, lat_half, NLON, C), jnp.bfloat16)], axis=1)
    shifted = jnp.roll(rolled, -lon_half, axis=2)
    windows = shifted.reshape(lev_blocks, WZ, lat_blocks, WY, lon_blocks, WX, C)
    windows = windows.transpose(2, 0, 4, 1, 3, 5, 6).reshape(lat_blocks, lev_blocks, lon_blocks, WIN, C)
    labels_win = region_ids.reshape(lat_blocks, WY, lon_blocks, WX).transpose(0, 2, 1, 3)
    labels_win = labels_win.reshape(lat_blocks, lon_blocks, WY * WX)
    labels_win = jnp.broadcast_to(labels_win[:, :, None, :], (lat_blocks, lon_blocks, WZ, WY * WX))
    labels_win = labels_win.reshape(lat_blocks, lon_blocks, WIN)
    token_pos = jnp.arange(WIN, dtype=jnp.int32)
    lat_offset = token_pos // WX % WY
    score_scale = 1.0 / head_dim ** 0.5

    def one_band(inputs):
        block, bias_band, labels_band, band_index = inputs
        projected = jnp.dot(block.reshape(-1, C), w_qkv, preferred_element_type=jnp.float32)
        projected = projected.astype(jnp.bfloat16).reshape(lev_blocks, lon_blocks, WIN, 3, HEADS, head_dim)
        queries = projected[:, :, :, 0].astype(jnp.float32)
        key_vecs = projected[:, :, :, 1].astype(jnp.float32)
        value_vecs = projected[:, :, :, 2].astype(jnp.float32)
        scores = jnp.einsum('zxqhd,zxkhd->zxhqk', queries, key_vecs) * score_scale
        scores = scores + bias_band.astype(jnp.float32)[None, None]
        valid_key = band_index * WY + lat_offset < NLAT - lat_half
        allowed = (labels_band[:, :, None] == labels_band[:, None, :]) & valid_key[None, None, :]
        scores = jnp.where(allowed[None, :, None], scores, -1000000000.0)
        attn_probs = jax.nn.softmax(scores, axis=-1).astype(jnp.bfloat16)
        context = jnp.einsum('zxhqk,zxkhd->zxqhd', attn_probs.astype(jnp.float32), value_vecs)
        context = context.astype(jnp.bfloat16).reshape(-1, C)
        mixed = jnp.dot(context, w_out, preferred_element_type=jnp.float32).astype(jnp.bfloat16)
        return mixed.reshape(lev_blocks, lon_blocks, WIN, C)
    band_ids = jnp.arange(lat_blocks, dtype=jnp.int32)
    mixed = lax.map(one_band, (windows, attn_bias, labels_win, band_ids))
    mixed = mixed.reshape(lat_blocks, lev_blocks, lon_blocks, WZ, WY, WX, C)
    mixed = mixed.transpose(1, 3, 0, 4, 2, 5, 6).reshape(NLEV, NLAT, NLON, C)
    returned = jnp.roll(mixed, lon_half, axis=2)
    returned = jnp.concatenate([jnp.zeros((NLEV, lat_half, NLON, C), jnp.bfloat16), returned[:, :NLAT - lat_half]], axis=1)
    returned = jnp.roll(returned, WZ // 2, axis=0)
    residual = state_field.astype(jnp.float32) + returned.astype(jnp.float32)
    normed_two = layer_norm(residual).astype(jnp.bfloat16)
    hidden = jax.nn.gelu(jnp.dot(normed_two.reshape(-1, C), w_up, preferred_element_type=jnp.float32))
    hidden = hidden.astype(jnp.bfloat16)
    update = jnp.dot(hidden, w_down, preferred_element_type=jnp.float32).reshape(residual.shape)
    return (residual + update).astype(jnp.bfloat16)
```

```python
import functools

import jax
import jax.numpy as jnp
from jax import lax
from jax.experimental import pallas as pl
from jax.experimental.pallas import tpu as pltpu
from jax.sharding import PartitionSpec as P

HEADS = 6
C = 192
FF = 768
HALF = 6
NB = 72
NC = 40
BC = NB + NC
EPS = 1e-05
NEG = -1000000000.0
SCALE = 1.0 / 32**0.5
MESH = pl.DeviceIdType.MESH
F32 = jnp.float32
BF16 = jnp.bfloat16

LON = (3 * BC, 176, 160)
LAT = (128, 64, 64)
RET = (6 * NC, 128, 112)


def dot(a, b):
    return jnp.dot(a, b, preferred_element_type=F32)


def dot_nt(a, b):
    return lax.dot_general(a, b, (((1,), (1,)), ((), ())), preferred_element_type=F32)


def dot_tt(a, b):
    return lax.dot_general(a, b, (((0,), (1,)), ((), ())), preferred_element_type=F32)


def layer_norm(values):
    average = jnp.mean(values, axis=-1, keepdims=True)
    centred = values - average
    variance = jnp.mean(centred * centred, axis=-1, keepdims=True)
    return centred * lax.rsqrt(variance + EPS)


def one_hot(hit):
    return jnp.where(hit, 1.0, 0.0).astype(BF16)


def iota(shape, axis):
    return lax.broadcasted_iota(jnp.int32, shape, axis)


def by36(t):
    return (t * 57) >> 11


def by18(t):
    return (t * 57) >> 10


def by6(t):
    return (t * 43) >> 8


def gather_of(side):
    t = iota((BC + NC, 1), 0)
    is_b = t < NB
    is_a = t >= BC
    u = jnp.where(is_a, t - BC, t - NB)
    lev = jnp.where(is_b, by36(t), by18(u))
    v = jnp.where(is_b, t - 36 * lev, u - 18 * lev)
    row = by6(v)
    col = v - 6 * row + HALF * side
    row = row + jnp.where(is_b, 3, jnp.where(is_a, 0, 9))
    source = lev * 192 + row * 16 + col
    source = jnp.where(is_b | (u < 36), source, -1)
    return one_hot(iota((BC + NC, 384), 1) == source)


def scatter_of(lev, rows, full):
    d = iota((rows * 16, 1), 0)
    row, col = d >> 4, d & 15
    side = jnp.where(col >= HALF, 1, 0)
    cc = col - HALF * side
    if full:
        at = jnp.where(row < 6, lev * 36 + row * 6 + cc, NB + lev * 18 + (row - 6) * 6 + cc)
        width = BC
    else:
        at = lev * 18 + row * 6 + cc
        width = NC
    source = jnp.where(col < 12, side * width + at, -1)
    return one_hot(iota((rows * 16, 2 * width), 1) == source)


def key_place(t, band, side):
    if band == 0:
        halo = t >= NB
        u = jnp.where(halo, t - NB, t)
        lev = by36(u)
        v = u - 36 * lev
        row = by6(v)
        col = v - 6 * row
        valid = t >= 0
    else:
        halo = t >= 2 * NC
        w = jnp.where(halo, t - 2 * NC, t)
        below = w >= NC
        u = jnp.where(below, w - NC, w)
        lev = by18(u)
        v = u - 18 * lev
        row = by6(v)
        col = v - 6 * row
        row = row + jnp.where(below, 3, 0)
        valid = u < 36
    col = col + jnp.where(halo, HALF * side, HALF * (1 - side))
    return lev, row, col, valid


def pack(buf, x, form):
    tokens, rest, second = form
    buf[0:tokens, :] = x[:, 0:128].astype(BF16)
    low, high = x[0:rest, 128:192], x[second : second + rest, 128:192]
    buf[tokens : tokens + rest, :] = jnp.concatenate([low, high], axis=1).astype(BF16)


def unpack(dst, buf, form):
    tokens, rest, second = form
    dst[0:tokens, 0:128] = buf[0:tokens, :]
    tail = buf[tokens : tokens + rest, :]
    dst[0:rest, 128:192] = tail[:, 0:64]
    dst[second : second + rest, 128:192] = tail[:, 64:128]


def attend(q, k, v, bias):
    n = q.shape[0]
    head = iota((1, C), 1) >> 5
    stacked = jnp.concatenate([jnp.where(head == h, q, 0.0) for h in range(HEADS)], axis=0)
    scores = dot_nt(stacked.astype(BF16), k) * SCALE + bias
    top = jnp.max(scores, axis=-1, keepdims=True)
    weights = jnp.exp(scores - top)
    total = jnp.sum(weights, axis=-1, keepdims=True)
    mixed = dot(weights.astype(BF16), v) * (1.0 / total)
    out = jnp.where(head == 0, mixed[0:n], 0.0)
    for h in range(1, HEADS):
        out = jnp.where(head == h, mixed[h * n : (h + 1) * n], out)
    return out


def feed_forward(residual, w_up, w_down):
    normed = layer_norm(residual).astype(BF16)
    hidden = jax.nn.gelu(dot(normed, w_up)).astype(BF16)
    return (residual + dot(hidden, w_down)).astype(BF16)


def kernel(
    n_lat,
    n_lon,
    state,
    attn_bias,
    region_ids,
    w_qkv,
    w_out,
    w_up,
    w_down,
    out,
    x_in,
    bias_in,
    region,
    region_left,
    wqkv_v,
    wq,
    wk,
    wv,
    wo_v,
    wu_v,
    wd_v,
    xp,
    st,
    normed,
    normed_a,
    m_lon,
    m_lat,
    m_ret,
    r_lon,
    r_lat,
    r_diag,
    r_ret,
    own_q,
    own_k,
    own_v,
    halo_x,
    lat_x,
    diag_x,
    halo_k,
    halo_v,
    lat_q,
    lat_k,
    lat_v,
    diag_k,
    diag_v,
    bias_b,
    bias_c,
    labels,
    mix,
    mix_ret,
    ret_x,
    out_bc,
    out_a,
    load_sem,
    send_sem,
    recv_sem,
):
    la = lax.axis_index("lat")
    lo = lax.axis_index("lon")
    right = lax.rem(lo + 1, n_lon)
    left = lax.rem(lo + n_lon - 1, n_lon)
    has_above = la > 0
    has_below = la < n_lat - 1

    barrier = pltpu.get_barrier_semaphore()
    for col in (left, right):
        pl.semaphore_signal(barrier, inc=1, device_id=(la, col), device_id_type=MESH)

    @pl.when(has_above)
    def _():
        for col in (left, lo, right):
            pl.semaphore_signal(barrier, inc=1, device_id=(la - 1, col), device_id_type=MESH)

    @pl.when(has_below)
    def _():
        for col in (left, lo, right):
            pl.semaphore_signal(barrier, inc=1, device_id=(la + 1, col), device_id_type=MESH)

    loads = [
        pltpu.make_async_copy(src, dst, load_sem.at[i])
        for i, (src, dst) in enumerate(
            [
                (state, x_in),
                (w_qkv, wqkv_v),
                (attn_bias, bias_in),
                (region_ids, region),
                (w_out, wo_v),
                (w_up, wu_v),
                (w_down, wd_v),
            ]
        )
    ]
    for load in loads:
        load.start()

    xp[...] = jnp.zeros_like(xp)
    normed_a[...] = jnp.zeros_like(normed_a)
    gathers = [gather_of(0), gather_of(1)]
    loads[0].wait()
    for lev in range(6):
        xp[lev, :, 0:12, :] = x_in[(lev + 1) % 6].astype(F32)
    for z in range(3):
        tokens = xp[2 * z : 2 * z + 2].reshape(384, C).astype(BF16)
        for side in range(2):
            x = dot(gathers[side], tokens)
            st[side, z] = x
            x = layer_norm(x)
            normed[side, z * BC : (z + 1) * BC, :] = x[0:BC]
            normed_a[side, z * NC : (z + 1) * NC, :] = x[BC : BC + NC]
    for side in range(2):
        pack(m_lon.at[side], normed[side], LON)
        pack(m_lat.at[side], normed_a[side], LAT)

    n_up = jnp.where(has_above, 3, 0)
    n_down = jnp.where(has_below, 3, 0)
    pl.semaphore_wait(barrier, 2 + n_up + n_down)

    def remote(src, dst, i, device):
        return pltpu.make_async_remote_copy(
            src_ref=src,
            dst_ref=dst,
            send_sem=send_sem.at[i],
            recv_sem=recv_sem.at[i],
            device_id=device,
            device_id_type=MESH,
        )

    to_left = remote(m_lon.at[0], r_lon.at[1], 0, (la, left))
    to_right = remote(m_lon.at[1], r_lon.at[0], 1, (la, right))
    regions = remote(region_ids, region_left, 2, (la, right))
    up = remote(m_lat, r_lat, 3, (la - 1, lo))
    up_left = remote(m_lat.at[0], r_diag.at[1], 4, (la - 1, left))
    up_right = remote(m_lat.at[1], r_diag.at[0], 5, (la - 1, right))
    down = remote(m_ret, r_ret, 6, (la + 1, lo))
    to_left.start()
    to_right.start()
    regions.start()

    @pl.when(has_above)
    def _():
        up_left.start()
        up_right.start()
        up.start()

    loads[1].wait()
    wq[...] = wqkv_v[:, 0:192]
    wk[...] = wqkv_v[:, 192:384]
    wv[...] = wqkv_v[:, 384:576]
    for side in range(2):
        x = normed[side].astype(BF16)
        own_q[side] = dot(x, wq[...])
        own_k[side] = dot(x, wk[...])
        own_v[side] = dot(x, wv[...])
    loads[2].wait()
    for band, (store, n, m) in enumerate(((bias_b, NB, 2 * NB), (bias_c, 2 * NC, 4 * NC))):
        for side in range(2):
            lev, row, col, valid = key_place(iota((m, 1), 0), band, side)
            at = jnp.where(valid, lev * 72 + row * 12 + col, -1)
            select = one_hot(iota((m, 144), 1) == at)
            rows = [dot(select[0:n], bias_in[band, h]) for h in range(HEADS)]
            rows = jnp.concatenate(rows, axis=0).astype(BF16)
            store[side] = dot_nt(rows, select)

    def apply_mask(side, source):
        labels[...] = jnp.zeros_like(labels)
        labels[0:12, 0:12] = source[...].astype(F32)
        table = labels[...].astype(BF16)
        for band, (store, n, m) in enumerate(((bias_b, NB, 2 * NB), (bias_c, 2 * NC, 4 * NC))):
            _, row, col, _ = key_place(iota((m, 1), 0), band, side)
            in_row = one_hot(iota((m, 16), 1) == row + 6 * band)
            queries = dot(in_row[0:n], table)
            queries = jnp.where(iota((n, 128), 1) == col[0:n], queries, 0.0)
            queries = jnp.sum(queries, axis=1, keepdims=True)
            _, row, col, valid = key_place(iota((1, m), 1), band, side)
            keys = dot_tt(table, in_row)
            keys = jnp.where(iota((128, m), 0) == col, keys, 0.0)
            keys = jnp.sum(keys, axis=0, keepdims=True)
            valid = valid & (la * 12 + 6 * band + row < n_lat * 12 - 3)
            keys = jnp.where(valid, keys, -1.0)
            allowed = queries == keys
            for h in range(HEADS):
                part = store[side, h * n : (h + 1) * n, :]
                store[side, h * n : (h + 1) * n, :] = jnp.where(allowed, part, NEG)

    loads[3].wait()
    apply_mask(1, region)

    regions.wait_recv()
    apply_mask(0, region_left)
    to_left.wait_recv()
    to_right.wait_recv()
    for side in range(2):
        unpack(halo_x.at[side], r_lon.at[side], LON)
        x = halo_x[side]
        halo_k[side] = dot(x, wk[...])
        halo_v[side] = dot(x, wv[...])

    @pl.when(has_below)
    def _():
        up.wait_recv()
        up_left.wait_recv()
        up_right.wait_recv()

    @pl.when(jnp.logical_not(has_below))
    def _():
        r_lat[...] = jnp.zeros_like(r_lat)
        r_diag[...] = jnp.zeros_like(r_diag)

    for side in range(2):
        unpack(lat_x.at[side], r_lat.at[side], LAT)
        unpack(diag_x.at[side], r_diag.at[side], LAT)
        x = lat_x[side]
        lat_q[side] = dot(x, wq[...])
        lat_k[side] = dot(x, wk[...])
        lat_v[side] = dot(x, wv[...])
        x = diag_x[side]
        diag_k[side] = dot(x, wk[...])
        diag_v[side] = dot(x, wv[...])

    loads[4].wait()

    def windows_c(z, carry):
        a = pl.ds(pl.multiple_of(z * NC, 8), NC)
        c = pl.ds(pl.multiple_of(z * BC + NB, 8), NC)
        for side in range(2):
            q = jnp.concatenate([own_q[side, c], lat_q[side, a]], axis=0)
            k = jnp.concatenate([own_k[side, c], lat_k[side, a], halo_k[side, c], diag_k[side, a]], axis=0)
            v = jnp.concatenate([own_v[side, c], lat_v[side, a], halo_v[side, c], diag_v[side, a]], axis=0)
            context = attend(q, k.astype(BF16), v.astype(BF16), bias_c[side])
            mixed = dot(context.astype(BF16), wo_v[...]).astype(BF16).astype(F32)
            mix[z, side, NB:BC, :] = mixed[0:NC]
            mix_ret[pl.ds(pl.multiple_of((z * 2 + side) * NC, 8), NC), :] = mixed[NC : 2 * NC]
        return carry

    lax.fori_loop(0, 3, windows_c, 0)
    pack(m_ret, mix_ret[...], RET)

    @pl.when(has_below)
    def _():
        down.start()

    def windows_b(z, carry):
        b = pl.ds(pl.multiple_of(z * BC, 8), NB)
        for side in range(2):
            k = jnp.concatenate([own_k[side, b], halo_k[side, b]], axis=0)
            v = jnp.concatenate([own_v[side, b], halo_v[side, b]], axis=0)
            context = attend(own_q[side, b], k.astype(BF16), v.astype(BF16), bias_b[side])
            mix[z, side, 0:NB, :] = dot(context.astype(BF16), wo_v[...]).astype(BF16).astype(F32)
        return carry

    lax.fori_loop(0, 3, windows_b, 0)
    loads[5].wait()
    loads[6].wait()

    for z in range(3):
        residual = jnp.concatenate([st[0, z, 0:BC] + mix[z, 0], st[1, z, 0:BC] + mix[z, 1]], axis=0)
        out_bc[...] = feed_forward(residual, wu_v[...], wd_v[...])
        for lev in range(2):
            grid = dot(scatter_of(lev, 9, True), out_bc[...]).reshape(9, 16, C)
            out[(2 * z + lev + 1) % 6, 3:12] = grid[:, 0:12, :].astype(BF16)

    @pl.when(has_above)
    def _():
        down.wait_recv()

    @pl.when(jnp.logical_not(has_above))
    def _():
        r_ret[...] = jnp.zeros_like(r_ret)

    unpack(ret_x, r_ret, RET)
    parts = [st[side, z, BC : BC + NC] for z in range(3) for side in range(2)]
    residual = jnp.concatenate(parts, axis=0) + ret_x[...].astype(F32)
    out_a[...] = feed_forward(residual, wu_v[...], wd_v[...])
    for z in range(3):
        for lev in range(2):
            grid = dot(scatter_of(lev, 3, False), out_a[z * 2 * NC : (z + 1) * 2 * NC, :]).reshape(3, 16, C)
            out[(2 * z + lev + 1) % 6, 0:3] = grid[:, 0:12, :].astype(BF16)

    to_left.wait_send()
    to_right.wait_send()
    regions.wait_send()

    @pl.when(has_above)
    def _():
        up_left.wait_send()
        up_right.wait_send()
        up.wait_send()

    @pl.when(has_below)
    def _():
        down.wait_send()


def shards(n_lat, n_lon, *args):
    def packed(form, *lead):
        return pltpu.VMEM((*lead, form[0] + form[1], 128), BF16)

    scratch = [
        pltpu.VMEM((6, 12, 12, C), BF16),
        pltpu.VMEM((2, HEADS, 144, 144), BF16),
        pltpu.VMEM((12, 12), jnp.int32),
        pltpu.VMEM((12, 12), jnp.int32),
        pltpu.VMEM((C, 3 * C), BF16),
        pltpu.VMEM((C, C), BF16),
        pltpu.VMEM((C, C), BF16),
        pltpu.VMEM((C, C), BF16),
        pltpu.VMEM((C, C), BF16),
        pltpu.VMEM((C, FF), BF16),
        pltpu.VMEM((FF, C), BF16),
        pltpu.VMEM((6, 12, 16, C), F32),
        pltpu.VMEM((2, 3, BC + NC, C), F32),
        pltpu.VMEM((2, 3 * BC, C), F32),
        pltpu.VMEM((2, 128, C), F32),
        packed(LON, 2),
        packed(LAT, 2),
        packed(RET),
        packed(LON, 2),
        packed(LAT, 2),
        packed(LAT, 2),
        packed(RET),
        pltpu.VMEM((2, 3 * BC, C), F32),
        pltpu.VMEM((2, 3 * BC, C), F32),
        pltpu.VMEM((2, 3 * BC, C), F32),
        pltpu.VMEM((2, 3 * BC, C), BF16),
        pltpu.VMEM((2, 128, C), BF16),
        pltpu.VMEM((2, 128, C), BF16),
        pltpu.VMEM((2, 3 * BC, C), F32),
        pltpu.VMEM((2, 3 * BC, C), F32),
        pltpu.VMEM((2, 128, C), F32),
        pltpu.VMEM((2, 128, C), F32),
        pltpu.VMEM((2, 128, C), F32),
        pltpu.VMEM((2, 128, C), F32),
        pltpu.VMEM((2, 128, C), F32),
        pltpu.VMEM((2, HEADS * NB, 2 * NB), F32),
        pltpu.VMEM((2, HEADS * 2 * NC, 4 * NC), F32),
        pltpu.VMEM((16, 128), F32),
        pltpu.VMEM((3, 2, BC, C), F32),
        pltpu.VMEM((6 * NC, C), F32),
        pltpu.VMEM((6 * NC, C), BF16),
        pltpu.VMEM((2 * BC, C), BF16),
        pltpu.VMEM((6 * NC, C), BF16),
        pltpu.SemaphoreType.DMA((7,)),
        pltpu.SemaphoreType.DMA((7,)),
        pltpu.SemaphoreType.DMA((7,)),
    ]
    return pl.pallas_call(
        functools.partial(kernel, n_lat, n_lon),
        out_shape=jax.ShapeDtypeStruct((6, 12, 12, C), BF16),
        in_specs=[pl.BlockSpec(memory_space=pltpu.HBM)] * 7,
        out_specs=pl.BlockSpec(memory_space=pltpu.VMEM),
        scratch_shapes=scratch,
        compiler_params=pltpu.CompilerParams(
            collective_id=0, has_side_effects=True, vmem_limit_bytes=40 * 1024 * 1024
        ),
    )(*args)


def solution(mesh):
    placed = (
        P(None, "lat", "lon", None),
        P("lat", None, None, None),
        P("lat", "lon"),
        P(),
        P(),
        P(),
        P(),
    )
    return jax.shard_map(
        functools.partial(shards, mesh.shape["lat"], mesh.shape["lon"]),
        mesh=mesh,
        in_specs=placed,
        out_specs=P(None, "lat", "lon", None),
        check_vma=False,
    )
```

```python
import functools

import jax
import jax.numpy as jnp
from jax import lax
from jax.experimental import pallas as pl
from jax.experimental.pallas import tpu as pltpu
from jax.sharding import PartitionSpec as P

HEADS = 6
C = 192
FF = 768
HALF = 6
NB = 72
NC = 40
BC = NB + NC
EPS = 1e-05
NEG = -1000000000.0
SCALE = 1.0 / 32**0.5
MESH = pl.DeviceIdType.MESH
F32 = jnp.float32
BF16 = jnp.bfloat16

LON = (3 * BC, 176, 160)
LAT = (128, 64, 64)
RET = (6 * NC, 128, 112)


def dot(a, b):
    return jnp.dot(a, b, preferred_element_type=F32)


def dot_nt(a, b):
    return lax.dot_general(a, b, (((1,), (1,)), ((), ())), preferred_element_type=F32)


def dot_tt(a, b):
    return lax.dot_general(a, b, (((0,), (1,)), ((), ())), preferred_element_type=F32)


def layer_norm(values):
    average = jnp.mean(values, axis=-1, keepdims=True)
    centred = values - average
    variance = jnp.mean(centred * centred, axis=-1, keepdims=True)
    return centred * lax.rsqrt(variance + EPS)


def one_hot(hit):
    return jnp.where(hit, 1.0, 0.0).astype(BF16)


def iota(shape, axis):
    return lax.broadcasted_iota(jnp.int32, shape, axis)


def by36(t):
    return (t * 57) >> 11


def by18(t):
    return (t * 57) >> 10


def by6(t):
    return (t * 43) >> 8


def gather_of(side):
    t = iota((BC + NC, 1), 0)
    is_b = t < NB
    is_a = t >= BC
    u = jnp.where(is_a, t - BC, t - NB)
    lev = jnp.where(is_b, by36(t), by18(u))
    v = jnp.where(is_b, t - 36 * lev, u - 18 * lev)
    row = by6(v)
    col = v - 6 * row + HALF * side
    row = row + jnp.where(is_b, 3, jnp.where(is_a, 0, 9))
    source = lev * 192 + row * 16 + col
    source = jnp.where(is_b | (u < 36), source, -1)
    return one_hot(iota((BC + NC, 384), 1) == source)


def scatter_of(lev, rows, full):
    d = iota((rows * 16, 1), 0)
    row, col = d >> 4, d & 15
    side = jnp.where(col >= HALF, 1, 0)
    cc = col - HALF * side
    if full:
        at = jnp.where(row < 6, lev * 36 + row * 6 + cc, NB + lev * 18 + (row - 6) * 6 + cc)
        width = BC
    else:
        at = lev * 18 + row * 6 + cc
        width = NC
    source = jnp.where(col < 12, side * width + at, -1)
    return one_hot(iota((rows * 16, 2 * width), 1) == source)


def key_place(t, band, side):
    if band == 0:
        halo = t >= NB
        u = jnp.where(halo, t - NB, t)
        lev = by36(u)
        v = u - 36 * lev
        row = by6(v)
        col = v - 6 * row
        valid = t >= 0
    else:
        halo = t >= 2 * NC
        w = jnp.where(halo, t - 2 * NC, t)
        below = w >= NC
        u = jnp.where(below, w - NC, w)
        lev = by18(u)
        v = u - 18 * lev
        row = by6(v)
        col = v - 6 * row
        row = row + jnp.where(below, 3, 0)
        valid = u < 36
    col = col + jnp.where(halo, HALF * side, HALF * (1 - side))
    return lev, row, col, valid


def pack(buf, x, form):
    tokens, rest, second = form
    buf[0:tokens, :] = x[:, 0:128].astype(BF16)
    low, high = x[0:rest, 128:192], x[second : second + rest, 128:192]
    buf[tokens : tokens + rest, :] = jnp.concatenate([low, high], axis=1).astype(BF16)


def unpack(dst, buf, form):
    tokens, rest, second = form
    dst[0:tokens, 0:128] = buf[0:tokens, :]
    tail = buf[tokens : tokens + rest, :]
    dst[0:rest, 128:192] = tail[:, 0:64]
    dst[second : second + rest, 128:192] = tail[:, 64:128]


def attend(q, k, v, bias):
    n = q.shape[0]
    head = iota((1, C), 1) >> 5
    stacked = jnp.concatenate([jnp.where(head == h, q, 0.0) for h in range(HEADS)], axis=0)
    scores = dot_nt(stacked.astype(BF16), k) * SCALE + bias
    top = jnp.max(scores, axis=-1, keepdims=True)
    weights = jnp.exp(scores - top)
    total = jnp.sum(weights, axis=-1, keepdims=True)
    mixed = dot(weights.astype(BF16), v) * (1.0 / total)
    out = jnp.where(head == 0, mixed[0:n], 0.0)
    for h in range(1, HEADS):
        out = jnp.where(head == h, mixed[h * n : (h + 1) * n], out)
    return out


def feed_forward(residual, w_up, w_down):
    normed = layer_norm(residual).astype(BF16)
    hidden = jax.nn.gelu(dot(normed, w_up)).astype(BF16)
    return (residual + dot_nt(hidden, w_down)).astype(BF16)


def kernel(
    n_lat,
    n_lon,
    state,
    attn_bias,
    region_ids,
    w_qkv,
    w_out,
    w_up,
    w_down,
    out,
    x_in,
    bias_in,
    region,
    region_left,
    wqkv_v,
    wq,
    wk,
    wv,
    wo_v,
    wu_v,
    wd_v,
    xp,
    st,
    normed,
    normed_a,
    m_lon,
    m_lat,
    m_ret,
    r_lon,
    r_lat,
    r_diag,
    r_ret,
    own_q,
    own_k,
    own_v,
    halo_x,
    lat_x,
    diag_x,
    halo_k,
    halo_v,
    lat_q,
    lat_k,
    lat_v,
    diag_k,
    diag_v,
    bias_b,
    bias_c,
    labels,
    mix,
    mix_ret,
    ret_x,
    out_bc,
    out_a,
    load_sem,
    send_sem,
    recv_sem,
):
    la = lax.axis_index("lat")
    lo = lax.axis_index("lon")
    right = lax.rem(lo + 1, n_lon)
    left = lax.rem(lo + n_lon - 1, n_lon)
    has_above = la > 0
    has_below = la < n_lat - 1

    barrier = pltpu.get_barrier_semaphore()
    for col in (left, right):
        pl.semaphore_signal(barrier, inc=1, device_id=(la, col), device_id_type=MESH)

    @pl.when(has_above)
    def _():
        for col in (left, lo, right):
            pl.semaphore_signal(barrier, inc=1, device_id=(la - 1, col), device_id_type=MESH)

    @pl.when(has_below)
    def _():
        for col in (left, lo, right):
            pl.semaphore_signal(barrier, inc=1, device_id=(la + 1, col), device_id_type=MESH)

    loads = [
        pltpu.make_async_copy(src, dst, load_sem.at[i])
        for i, (src, dst) in enumerate(
            [
                (state, x_in),
                (w_qkv, wqkv_v),
                (attn_bias, bias_in),
                (region_ids, region),
                (w_out, wo_v),
                (w_up, wu_v),
                (w_down, wd_v),
            ]
        )
    ]
    for load in loads:
        load.start()

    xp[...] = jnp.zeros_like(xp)
    normed_a[...] = jnp.zeros_like(normed_a)
    gathers = [gather_of(0), gather_of(1)]
    loads[0].wait()
    for lev in range(6):
        xp[lev, :, 0:12, :] = x_in[(lev + 1) % 6].astype(F32)
    for z in range(3):
        tokens = xp[2 * z : 2 * z + 2].reshape(384, C).astype(BF16)
        for side in range(2):
            x = dot(gathers[side], tokens)
            st[side, z] = x
            x = layer_norm(x)
            normed[side, z * BC : (z + 1) * BC, :] = x[0:BC]
            normed_a[side, z * NC : (z + 1) * NC, :] = x[BC : BC + NC]
    for side in range(2):
        pack(m_lon.at[side], normed[side], LON)
        pack(m_lat.at[side], normed_a[side], LAT)

    n_up = jnp.where(has_above, 3, 0)
    n_down = jnp.where(has_below, 3, 0)
    pl.semaphore_wait(barrier, 2 + n_up + n_down)

    def remote(src, dst, i, device):
        return pltpu.make_async_remote_copy(
            src_ref=src,
            dst_ref=dst,
            send_sem=send_sem.at[i],
            recv_sem=recv_sem.at[i],
            device_id=device,
            device_id_type=MESH,
        )

    to_left = remote(m_lon.at[0], r_lon.at[1], 0, (la, left))
    to_right = remote(m_lon.at[1], r_lon.at[0], 1, (la, right))
    regions = remote(region_ids, region_left, 2, (la, right))
    up = remote(m_lat, r_lat, 3, (la - 1, lo))
    up_left = remote(m_lat.at[0], r_diag.at[1], 4, (la - 1, left))
    up_right = remote(m_lat.at[1], r_diag.at[0], 5, (la - 1, right))
    down = remote(m_ret, r_ret, 6, (la + 1, lo))
    to_left.start()
    to_right.start()
    regions.start()

    @pl.when(has_above)
    def _():
        up_left.start()
        up_right.start()
        up.start()

    loads[1].wait()
    wq[...] = wqkv_v[:, 0:192]
    wk[...] = wqkv_v[:, 192:384]
    wv[...] = wqkv_v[:, 384:576]
    for side in range(2):
        x = normed[side].astype(BF16)
        own_q[side] = dot(x, wq[...])
        own_k[side] = dot(x, wk[...])
        own_v[side] = dot(x, wv[...])
    loads[2].wait()
    for band, (store, n, m) in enumerate(((bias_b, NB, 2 * NB), (bias_c, 2 * NC, 4 * NC))):
        for side in range(2):
            lev, row, col, valid = key_place(iota((m, 1), 0), band, side)
            at = jnp.where(valid, lev * 72 + row * 12 + col, -1)
            select = one_hot(iota((m, 144), 1) == at)
            rows = [dot(select[0:n], bias_in[band, h]) for h in range(HEADS)]
            rows = jnp.concatenate(rows, axis=0).astype(BF16)
            store[side] = dot_nt(rows, select)

    def apply_mask(side, source):
        labels[...] = jnp.zeros_like(labels)
        labels[0:12, 0:12] = source[...].astype(F32)
        table = labels[...].astype(BF16)
        for band, (store, n, m) in enumerate(((bias_b, NB, 2 * NB), (bias_c, 2 * NC, 4 * NC))):
            _, row, col, _ = key_place(iota((m, 1), 0), band, side)
            in_row = one_hot(iota((m, 16), 1) == row + 6 * band)
            queries = dot(in_row[0:n], table)
            queries = jnp.where(iota((n, 128), 1) == col[0:n], queries, 0.0)
            queries = jnp.sum(queries, axis=1, keepdims=True)
            _, row, col, valid = key_place(iota((1, m), 1), band, side)
            keys = dot_tt(table, in_row)
            keys = jnp.where(iota((128, m), 0) == col, keys, 0.0)
            keys = jnp.sum(keys, axis=0, keepdims=True)
            valid = valid & (la * 12 + 6 * band + row < n_lat * 12 - 3)
            keys = jnp.where(valid, keys, -1.0)
            allowed = queries == keys
            for h in range(HEADS):
                part = store[side, h * n : (h + 1) * n, :]
                store[side, h * n : (h + 1) * n, :] = jnp.where(allowed, part, NEG)

    loads[3].wait()
    apply_mask(1, region)

    regions.wait_recv()
    apply_mask(0, region_left)
    to_left.wait_recv()
    to_right.wait_recv()
    for side in range(2):
        unpack(halo_x.at[side], r_lon.at[side], LON)
        x = halo_x[side]
        halo_k[side] = dot(x, wk[...])
        halo_v[side] = dot(x, wv[...])

    @pl.when(has_below)
    def _():
        up.wait_recv()
        up_left.wait_recv()
        up_right.wait_recv()

    @pl.when(jnp.logical_not(has_below))
    def _():
        r_lat[...] = jnp.zeros_like(r_lat)
        r_diag[...] = jnp.zeros_like(r_diag)

    for side in range(2):
        unpack(lat_x.at[side], r_lat.at[side], LAT)
        unpack(diag_x.at[side], r_diag.at[side], LAT)
        x = lat_x[side]
        lat_q[side] = dot(x, wq[...])
        lat_k[side] = dot(x, wk[...])
        lat_v[side] = dot(x, wv[...])
        x = diag_x[side]
        diag_k[side] = dot(x, wk[...])
        diag_v[side] = dot(x, wv[...])

    loads[4].wait()

    def windows_c(z, carry):
        a = pl.ds(pl.multiple_of(z * NC, 8), NC)
        c = pl.ds(pl.multiple_of(z * BC + NB, 8), NC)
        for side in range(2):
            q = jnp.concatenate([own_q[side, c], lat_q[side, a]], axis=0)
            k = jnp.concatenate([own_k[side, c], lat_k[side, a], halo_k[side, c], diag_k[side, a]], axis=0)
            v = jnp.concatenate([own_v[side, c], lat_v[side, a], halo_v[side, c], diag_v[side, a]], axis=0)
            context = attend(q, k.astype(BF16), v.astype(BF16), bias_c[side])
            mixed = dot(context.astype(BF16), wo_v[...]).astype(BF16).astype(F32)
            mix[z, side, NB:BC, :] = mixed[0:NC]
            mix_ret[pl.ds(pl.multiple_of((z * 2 + side) * NC, 8), NC), :] = mixed[NC : 2 * NC]
        return carry

    lax.fori_loop(0, 3, windows_c, 0)
    pack(m_ret, mix_ret[...], RET)

    @pl.when(has_below)
    def _():
        down.start()

    def windows_b(z, carry):
        b = pl.ds(pl.multiple_of(z * BC, 8), NB)
        for side in range(2):
            k = jnp.concatenate([own_k[side, b], halo_k[side, b]], axis=0)
            v = jnp.concatenate([own_v[side, b], halo_v[side, b]], axis=0)
            context = attend(own_q[side, b], k.astype(BF16), v.astype(BF16), bias_b[side])
            mix[z, side, 0:NB, :] = dot(context.astype(BF16), wo_v[...]).astype(BF16).astype(F32)
        return carry

    lax.fori_loop(0, 3, windows_b, 0)
    loads[5].wait()
    loads[6].wait()

    for z in range(3):
        residual = jnp.concatenate([st[0, z, 0:BC] + mix[z, 0], st[1, z, 0:BC] + mix[z, 1]], axis=0)
        out_bc[...] = feed_forward(residual, wu_v[...], wd_v[...])
        for lev in range(2):
            grid = dot(scatter_of(lev, 9, True), out_bc[...]).reshape(9, 16, C)
            out[(2 * z + lev + 1) % 6, 3:12] = grid[:, 0:12, :].astype(BF16)

    @pl.when(has_above)
    def _():
        down.wait_recv()

    @pl.when(jnp.logical_not(has_above))
    def _():
        r_ret[...] = jnp.zeros_like(r_ret)

    unpack(ret_x, r_ret, RET)
    parts = [st[side, z, BC : BC + NC] for z in range(3) for side in range(2)]
    residual = jnp.concatenate(parts, axis=0) + ret_x[...].astype(F32)
    out_a[...] = feed_forward(residual, wu_v[...], wd_v[...])
    for z in range(3):
        for lev in range(2):
            grid = dot(scatter_of(lev, 3, False), out_a[z * 2 * NC : (z + 1) * 2 * NC, :]).reshape(3, 16, C)
            out[(2 * z + lev + 1) % 6, 0:3] = grid[:, 0:12, :].astype(BF16)

    to_left.wait_send()
    to_right.wait_send()
    regions.wait_send()

    @pl.when(has_above)
    def _():
        up_left.wait_send()
        up_right.wait_send()
        up.wait_send()

    @pl.when(has_below)
    def _():
        down.wait_send()


def shards(n_lat, n_lon, *args):
    args = (*args[:6], args[6].T)
    args = [pltpu.with_memory_space_constraint(a, pltpu.HBM) for a in args]
    def packed(form, *lead):
        return pltpu.VMEM((*lead, form[0] + form[1], 128), BF16)

    scratch = [
        pltpu.VMEM((6, 12, 12, C), BF16),
        pltpu.VMEM((2, HEADS, 144, 144), BF16),
        pltpu.VMEM((12, 12), jnp.int32),
        pltpu.VMEM((12, 12), jnp.int32),
        pltpu.VMEM((C, 3 * C), BF16),
        pltpu.VMEM((C, C), BF16),
        pltpu.VMEM((C, C), BF16),
        pltpu.VMEM((C, C), BF16),
        pltpu.VMEM((C, C), BF16),
        pltpu.VMEM((C, FF), BF16),
        pltpu.VMEM((C, FF), BF16),
        pltpu.VMEM((6, 12, 16, C), F32),
        pltpu.VMEM((2, 3, BC + NC, C), F32),
        pltpu.VMEM((2, 3 * BC, C), F32),
        pltpu.VMEM((2, 128, C), F32),
        packed(LON, 2),
        packed(LAT, 2),
        packed(RET),
        packed(LON, 2),
        packed(LAT, 2),
        packed(LAT, 2),
        packed(RET),
        pltpu.VMEM((2, 3 * BC, C), F32),
        pltpu.VMEM((2, 3 * BC, C), F32),
        pltpu.VMEM((2, 3 * BC, C), F32),
        pltpu.VMEM((2, 3 * BC, C), BF16),
        pltpu.VMEM((2, 128, C), BF16),
        pltpu.VMEM((2, 128, C), BF16),
        pltpu.VMEM((2, 3 * BC, C), F32),
        pltpu.VMEM((2, 3 * BC, C), F32),
        pltpu.VMEM((2, 128, C), F32),
        pltpu.VMEM((2, 128, C), F32),
        pltpu.VMEM((2, 128, C), F32),
        pltpu.VMEM((2, 128, C), F32),
        pltpu.VMEM((2, 128, C), F32),
        pltpu.VMEM((2, HEADS * NB, 2 * NB), F32),
        pltpu.VMEM((2, HEADS * 2 * NC, 4 * NC), F32),
        pltpu.VMEM((16, 128), F32),
        pltpu.VMEM((3, 2, BC, C), F32),
        pltpu.VMEM((6 * NC, C), F32),
        pltpu.VMEM((6 * NC, C), BF16),
        pltpu.VMEM((2 * BC, C), BF16),
        pltpu.VMEM((6 * NC, C), BF16),
        pltpu.SemaphoreType.DMA((7,)),
        pltpu.SemaphoreType.DMA((7,)),
        pltpu.SemaphoreType.DMA((7,)),
    ]
    return pl.pallas_call(
        functools.partial(kernel, n_lat, n_lon),
        out_shape=pltpu.VMEM((6, 12, 12, C), BF16),
        in_specs=[pl.BlockSpec(memory_space=pltpu.HBM)] * 7,
        out_specs=pl.BlockSpec(memory_space=pltpu.VMEM),
        scratch_shapes=scratch,
        compiler_params=pltpu.CompilerParams(
            collective_id=0, has_side_effects=True, vmem_limit_bytes=40 * 1024 * 1024
        ),
    )(*args)


def solution(mesh):
    placed = (
        P(None, "lat", "lon", None),
        P("lat", None, None, None),
        P("lat", "lon"),
        P(),
        P(),
        P(),
        P(),
    )
    return jax.shard_map(
        functools.partial(shards, mesh.shape["lat"], mesh.shape["lon"]),
        mesh=mesh,
        in_specs=placed,
        out_specs=P(None, "lat", "lon", None),
        check_vma=False,
    )
```

```python
import functools

import jax
import jax.numpy as jnp
from jax import lax
from jax.experimental import pallas as pl
from jax.experimental.pallas import tpu as pltpu
from jax.sharding import PartitionSpec as P

HEADS = 6
C = 192
FF = 768
HALF = 6
NB = 72
NC = 40
BC = NB + NC
EPS = 1e-05
NEG = -1000000000.0
SCALE = 1.0 / 32**0.5
MESH = pl.DeviceIdType.MESH
F32 = jnp.float32
BF16 = jnp.bfloat16

LON = (3 * BC, 176, 160)
LAT = (128, 64, 64)


def dot(a, b):
    return jnp.dot(a, b, preferred_element_type=F32)


def dot_nt(a, b):
    return lax.dot_general(a, b, (((1,), (1,)), ((), ())), preferred_element_type=F32)


def dot_tt(a, b):
    return lax.dot_general(a, b, (((0,), (1,)), ((), ())), preferred_element_type=F32)


def dot_tn(a, b):
    return lax.dot_general(a, b, (((0,), (0,)), ((), ())), preferred_element_type=F32)


def layer_norm(values):
    average = jnp.mean(values, axis=-1, keepdims=True)
    centred = values - average
    variance = jnp.mean(centred * centred, axis=-1, keepdims=True)
    return centred * lax.rsqrt(variance + EPS)


def one_hot(hit):
    return jnp.where(hit, 1.0, 0.0).astype(BF16)


def iota(shape, axis):
    return lax.broadcasted_iota(jnp.int32, shape, axis)


def by36(t):
    return (t * 57) >> 11


def by18(t):
    return (t * 57) >> 10


def by6(t):
    return (t * 43) >> 8


def gather_of(side):
    t = iota((BC + NC, 1), 0)
    is_b = t < NB
    is_a = t >= BC
    u = jnp.where(is_a, t - BC, t - NB)
    lev = jnp.where(is_b, by36(t), by18(u))
    v = jnp.where(is_b, t - 36 * lev, u - 18 * lev)
    row = by6(v)
    col = v - 6 * row + HALF * side
    row = row + jnp.where(is_b, 3, jnp.where(is_a, 0, 9))
    source = lev * 192 + row * 16 + col
    source = jnp.where(is_b | (u < 36), source, -1)
    return one_hot(iota((BC + NC, 384), 1) == source)


def scatter_of(lev, rows, full):
    d = iota((rows * 16, 1), 0)
    row, col = d >> 4, d & 15
    side = jnp.where(col >= HALF, 1, 0)
    cc = col - HALF * side
    if full:
        at = jnp.where(row < 6, lev * 36 + row * 6 + cc, NB + lev * 18 + (row - 6) * 6 + cc)
        width = BC
    else:
        at = lev * 18 + row * 6 + cc
        width = NC
    source = jnp.where(col < 12, side * width + at, -1)
    return one_hot(iota((rows * 16, 2 * width), 1) == source)


def key_place(t, band, side):
    if band == 0:
        halo = t >= NB
        u = jnp.where(halo, t - NB, t)
        lev = by36(u)
        v = u - 36 * lev
        row = by6(v)
        col = v - 6 * row
        valid = t >= 0
    else:
        halo = t >= 2 * NC
        w = jnp.where(halo, t - 2 * NC, t)
        below = w >= NC
        u = jnp.where(below, w - NC, w)
        lev = by18(u)
        v = u - 18 * lev
        row = by6(v)
        col = v - 6 * row
        row = row + jnp.where(below, 3, 0)
        valid = u < 36
    col = col + jnp.where(halo, HALF * side, HALF * (1 - side))
    return lev, row, col, valid


def pack(buf, x, form):
    tokens, rest, second = form
    buf[0:tokens, :] = x[:, 0:128].astype(BF16)
    low, high = x[0:rest, 128:192], x[second : second + rest, 128:192]
    buf[tokens : tokens + rest, :] = jnp.concatenate([low, high], axis=1).astype(BF16)


def unpack(dst, buf, form):
    tokens, rest, second = form
    dst[0:tokens, 0:128] = buf[0:tokens, :]
    tail = buf[tokens : tokens + rest, :]
    dst[0:rest, 128:192] = tail[:, 0:64]
    dst[second : second + rest, 128:192] = tail[:, 64:128]


def attend(q, k, v, bias):
    n = q.shape[0]
    head = iota((1, C), 1) >> 5
    stacked = jnp.concatenate([jnp.where(head == h, q, 0.0) for h in range(HEADS)], axis=0)
    scores = dot_nt(stacked.astype(BF16), k) * SCALE + bias
    top = jnp.max(scores, axis=-1, keepdims=True)
    weights = jnp.exp(scores - top)
    total = jnp.sum(weights, axis=-1, keepdims=True)
    mixed = dot(weights.astype(BF16), v) * (1.0 / total)
    out = jnp.where(head == 0, mixed[0:n], 0.0)
    for h in range(1, HEADS):
        out = jnp.where(head == h, mixed[h * n : (h + 1) * n], out)
    return out


def feed_forward(residual, w_up, w_down):
    normed = layer_norm(residual).astype(BF16)
    hidden = jax.nn.gelu(dot(normed, w_up)).astype(BF16)
    return residual + dot_nt(hidden, w_down)


def kernel(
    n_lat,
    n_lon,
    state,
    attn_bias,
    region_ids,
    w_qkv,
    w_out,
    w_up,
    w_down,
    out,
    x_in,
    bias_in,
    region,
    region_left,
    wqkv_v,
    wq,
    wk,
    wv,
    wo_v,
    wu_v,
    wd_v,
    xp,
    st,
    normed,
    normed_a,
    m_lon,
    m_lat,
    m_ret,
    r_lon,
    r_lat,
    r_diag,
    r_ret,
    own_q,
    own_k,
    own_v,
    halo_x,
    lat_x,
    diag_x,
    halo_k,
    halo_v,
    lat_q,
    lat_k,
    lat_v,
    diag_k,
    diag_v,
    bias_b,
    bias_c,
    labels,
    mix,
    mix_ret,
    ret_x,
    out_bc,
    out_a,
    load_sem,
    send_sem,
    recv_sem,
    here_sem,
):
    la = lax.axis_index("lat")
    lo = lax.axis_index("lon")
    right = lax.rem(lo + 1, n_lon)
    left = lax.rem(lo + n_lon - 1, n_lon)
    has_above = la > 0
    has_below = la < n_lat - 1
    half = n_lon // 2
    far_left = lax.rem(lo, half) == 0
    far_right = lax.rem(lo + 1, half) == 0
    end = far_left | far_right
    end_on_left = lax.rem(lo + half - 1, half) == 0
    end_on_right = lax.rem(lo + 2, half) == 0
    mate = end_on_left | end_on_right
    near = jnp.where(far_left, right, jnp.where(far_right, left, lo))
    sides = ((far_left, left), (far_right, right))

    barrier = pltpu.get_barrier_semaphore()

    def greet(row, col):
        pl.semaphore_signal(barrier, inc=1, device_id=(row, col), device_id_type=MESH)

    pl.when(jnp.logical_not(end_on_left))(functools.partial(greet, la, left))
    pl.when(jnp.logical_not(end_on_right))(functools.partial(greet, la, right))
    for there, row in ((has_above, la - 1), (has_below, la + 1)):
        pl.when(there)(functools.partial(greet, row, near))
        for far, col in sides:
            pl.when(there & far)(functools.partial(greet, row, col))

    loads = [
        pltpu.make_async_copy(src, dst, load_sem.at[i])
        for i, (src, dst) in enumerate(
            [
                (state, x_in),
                (w_qkv, wqkv_v),
                (attn_bias, bias_in),
                (region_ids, region),
                (w_out, wo_v),
                (w_up, wu_v),
                (w_down, wd_v),
            ]
        )
    ]
    for load in loads:
        load.start()

    xp[...] = jnp.zeros_like(xp)
    normed_a[...] = jnp.zeros_like(normed_a)
    mix_ret[...] = jnp.zeros_like(mix_ret)
    gathers = [gather_of(0), gather_of(1)]
    loads[0].wait()
    for lev in range(6):
        xp[lev, :, 0:12, :] = x_in[(lev + 1) % 6].astype(F32)
    for z in range(3):
        tokens = xp[2 * z : 2 * z + 2].reshape(384, C).astype(BF16)
        for side in range(2):
            x = dot(gathers[side], tokens)
            st[side, z] = x
            x = layer_norm(x)
            normed[side, z * BC : (z + 1) * BC, :] = x[0:BC]
            normed_a[side, z * NC : (z + 1) * NC, :] = x[BC : BC + NC]
    for side in range(2):
        pack(m_lon.at[side], normed[side], LON)
        pack(m_lat.at[side], normed_a[side], LAT)

    def remote(src, dst, i, device):
        return pltpu.make_async_remote_copy(
            src_ref=src,
            dst_ref=dst,
            send_sem=send_sem.at[i],
            recv_sem=recv_sem.at[i],
            device_id=device,
            device_id_type=MESH,
        )

    def along(side, col):
        return remote(m_lon.at[side], r_lon.at[1 - side], 1 - side, (la, col))

    def corner(side, source, row, col):
        return remote(source.at[side], r_diag.at[1 - side], 3 - side, (row, col))

    regions = remote(region_ids, region_left, 4, (la, right))
    up = remote(m_lat, r_lat, 5, (la - 1, lo))

    rows = jnp.where(has_above, 1, 0) + jnp.where(has_below, 1, 0)

    def send_near():
        @pl.when(jnp.logical_not(end))
        def _():
            pl.semaphore_wait(barrier, 2 + rows * jnp.where(mate, 2, 1))

        @pl.when(mate)
        def _():
            col = jnp.where(end_on_left, left, right)
            pl.semaphore_signal(here_sem, inc=1, device_id=(la, col), device_id_type=MESH)

        @pl.when(end)
        def _():
            pl.semaphore_wait(here_sem, 1)

        pl.when(has_above)(up.start)
        pl.when(jnp.logical_not(far_right))(regions.start)
        for side, (far, col) in enumerate(sides):
            pl.when(jnp.logical_not(far))(along(side, col).start)

    def send_far():
        pl.semaphore_wait(barrier, 1 + rows)
        pl.when(far_right)(regions.start)
        for side, (far, col) in enumerate(sides):
            pl.when(far & has_above)(corner(side, m_lat, la - 1, col).start)
            pl.when(far)(along(side, col).start)

    def prepare():
        loads[1].wait()
        wq[...] = wqkv_v[:, 0:192]
        wk[...] = wqkv_v[:, 192:384]
        wv[...] = wqkv_v[:, 384:576]
        for side in range(2):
            x = normed[side].astype(BF16)
            own_q[side] = dot(x, wq[...])
            own_k[side] = dot(x, wk[...])
            own_v[side] = dot(x, wv[...])
        loads[2].wait()
        for band, (store, n, m) in enumerate(((bias_b, NB, 2 * NB), (bias_c, 2 * NC, 4 * NC))):
            for side in range(2):
                lev, row, col, valid = key_place(iota((m, 1), 0), band, side)
                at = jnp.where(valid, lev * 72 + row * 12 + col, -1)
                select = one_hot(iota((m, 144), 1) == at)
                rows = [dot(select[0:n], bias_in[band, h]) for h in range(HEADS)]
                rows = jnp.concatenate(rows, axis=0).astype(BF16)
                store[side] = dot_nt(rows, select)
        loads[3].wait()
        apply_mask(1, region)

    def apply_mask(side, source):
        labels[...] = jnp.zeros_like(labels)
        labels[0:12, 0:12] = source[...].astype(F32)
        table = labels[...].astype(BF16)
        for band, (store, n, m) in enumerate(((bias_b, NB, 2 * NB), (bias_c, 2 * NC, 4 * NC))):
            _, row, col, _ = key_place(iota((m, 1), 0), band, side)
            in_row = one_hot(iota((m, 16), 1) == row + 6 * band)
            queries = dot(in_row[0:n], table)
            queries = jnp.where(iota((n, 128), 1) == col[0:n], queries, 0.0)
            queries = jnp.sum(queries, axis=1, keepdims=True)
            _, row, col, valid = key_place(iota((1, m), 1), band, side)
            keys = dot_tt(table, in_row)
            keys = jnp.where(iota((128, m), 0) == col, keys, 0.0)
            keys = jnp.sum(keys, axis=0, keepdims=True)
            valid = valid & (la * 12 + 6 * band + row < n_lat * 12 - 3)
            keys = jnp.where(valid, keys, -1.0)
            allowed = queries == keys
            for h in range(HEADS):
                part = store[side, h * n : (h + 1) * n, :]
                store[side, h * n : (h + 1) * n, :] = jnp.where(allowed, part, NEG)

    def start(i, carry):
        far_first = lo >= half
        pl.when(i == jnp.where(far_first, 1, 0))(send_near)
        pl.when(end & (i == jnp.where(far_first, 0, 2)))(send_far)
        pl.when(i == jnp.where(far_first, 2, 1))(prepare)
        return carry

    lax.fori_loop(0, 3, start, 0)

    @pl.when(has_below)
    def _():
        up.wait_recv()
        for side, (far, col) in enumerate(sides):
            pl.when(jnp.logical_not(far))(corner(side, r_lat, la, col).start)

    @pl.when(jnp.logical_not(has_below))
    def _():
        r_lat[...] = jnp.zeros_like(r_lat)
        r_diag[...] = jnp.zeros_like(r_diag)

    for side in range(2):
        unpack(lat_x.at[side], r_lat.at[side], LAT)
        x = lat_x[side]
        lat_q[side] = dot(x, wq[...])
        lat_k[side] = dot(x, wk[...])
        lat_v[side] = dot(x, wv[...])
    loads[4].wait()
    loads[5].wait()
    loads[6].wait()

    def window_column(i, carry):
        side = jnp.where(far_left, 1 - i, i)

        @pl.when(side == 0)
        def _():
            regions.wait_recv()
            apply_mask(0, region_left)

        along(1 - side, left).wait_recv()
        unpack(halo_x, r_lon.at[side], LON)
        x = halo_x[...]
        halo_k[...] = dot(x, wk[...])
        halo_v[...] = dot(x, wv[...])

        @pl.when(has_below)
        def _():
            corner(1 - side, r_lat, la, left).wait_recv()

        unpack(diag_x, r_diag.at[side], LAT)
        x = diag_x[...]
        diag_k[...] = dot(x, wk[...])
        diag_v[...] = dot(x, wv[...])

        for z in range(3):
            a = pl.ds(z * NC, NC)
            c = pl.ds(z * BC + NB, NC)
            q = jnp.concatenate([own_q[side, c], lat_q[side, a]], axis=0)
            k = jnp.concatenate([own_k[side, c], lat_k[side, a], halo_k[c], diag_k[a]], axis=0)
            v = jnp.concatenate([own_v[side, c], lat_v[side, a], halo_v[c], diag_v[a]], axis=0)
            context = attend(q, k.astype(BF16), v.astype(BF16), bias_c[side])
            mixed = dot(context.astype(BF16), wo_v[...]).astype(BF16).astype(F32)
            mix[z * BC + NB : (z + 1) * BC, :] = mixed[0:NC]
            mix_ret[z * NC : (z + 1) * NC, :] = mixed[NC : 2 * NC]
        pack(m_ret.at[side], mix_ret[...], LAT)

        @pl.when(has_below)
        def _():
            down(side).start()

        for z in range(3):
            b = pl.ds(z * BC, NB)
            k = jnp.concatenate([own_k[side, b], halo_k[b]], axis=0)
            v = jnp.concatenate([own_v[side, b], halo_v[b]], axis=0)
            context = attend(own_q[side, b], k.astype(BF16), v.astype(BF16), bias_b[side])
            mix[z * BC : z * BC + NB, :] = dot(context.astype(BF16), wo_v[...]).astype(BF16).astype(F32)
        residual = jnp.concatenate([st[side, z, 0:BC] for z in range(3)], axis=0) + mix[...]
        out_bc[side] = feed_forward(residual, wu_v[...], wd_v[...]).astype(BF16)
        return carry

    def down(side):
        return remote(m_ret.at[side], r_ret.at[side], 6 + side, (la + 1, lo))

    lax.fori_loop(0, 2, window_column, 0)

    for lev in range(2):
        scatter = scatter_of(lev, 9, True)
        for z in range(3):
            part = pl.ds(z * BC, BC)
            grid = dot(scatter, jnp.concatenate([out_bc[0, part], out_bc[1, part]], axis=0)).reshape(9, 16, C)
            out[(2 * z + lev + 1) % 6, 3:12] = grid[:, 0:12, :].astype(BF16)

    @pl.when(has_above)
    def _():
        down(0).wait_recv()
        down(1).wait_recv()

    @pl.when(jnp.logical_not(has_above))
    def _():
        r_ret[...] = jnp.zeros_like(r_ret)

    for side in range(2):
        unpack(ret_x.at[side], r_ret.at[side], LAT)
    residual = [
        st[side, z, BC : BC + NC] + ret_x[side, z * NC : (z + 1) * NC, :].astype(F32) for z in range(3) for side in range(2)
    ]
    out_a[...] = feed_forward(jnp.concatenate(residual, axis=0), wu_v[...], wd_v[...]).astype(BF16)
    for lev in range(2):
        scatter = scatter_of(lev, 3, False)
        for z in range(3):
            grid = dot(scatter, out_a[z * 2 * NC : (z + 1) * 2 * NC, :]).reshape(3, 16, C)
            out[(2 * z + lev + 1) % 6, 0:3] = grid[:, 0:12, :].astype(BF16)

    along(0, left).wait_send()
    along(1, right).wait_send()
    regions.wait_send()

    @pl.when(has_above)
    def _():
        for side, (far, col) in enumerate(sides):
            pl.when(far)(corner(side, m_lat, la - 1, col).wait_send)
        up.wait_send()

    @pl.when(has_below)
    def _():
        for side, (far, col) in enumerate(sides):
            pl.when(jnp.logical_not(far))(corner(side, r_lat, la, col).wait_send)
        down(0).wait_send()
        down(1).wait_send()


def shards(n_lat, n_lon, *args):
    args = (*args[:6], args[6].T)
    args = [pltpu.with_memory_space_constraint(a, pltpu.HBM) for a in args]
    def packed(form, *lead):
        return pltpu.VMEM((*lead, form[0] + form[1], 128), BF16)

    scratch = [
        pltpu.VMEM((6, 12, 12, C), BF16),
        pltpu.VMEM((2, HEADS, 144, 144), BF16),
        pltpu.VMEM((12, 12), jnp.int32),
        pltpu.VMEM((12, 12), jnp.int32),
        pltpu.VMEM((C, 3 * C), BF16),
        pltpu.VMEM((C, C), BF16),
        pltpu.VMEM((C, C), BF16),
        pltpu.VMEM((C, C), BF16),
        pltpu.VMEM((C, C), BF16),
        pltpu.VMEM((C, FF), BF16),
        pltpu.VMEM((C, FF), BF16),
        pltpu.VMEM((6, 12, 16, C), F32),
        pltpu.VMEM((2, 3, BC + NC, C), F32),
        pltpu.VMEM((2, 3 * BC, C), F32),
        pltpu.VMEM((2, 128, C), F32),
        packed(LON, 2),
        packed(LAT, 2),
        packed(LAT, 2),
        packed(LON, 2),
        packed(LAT, 2),
        packed(LAT, 2),
        packed(LAT, 2),
        pltpu.VMEM((2, 3 * BC, C), F32),
        pltpu.VMEM((2, 3 * BC, C), F32),
        pltpu.VMEM((2, 3 * BC, C), F32),
        pltpu.VMEM((3 * BC, C), BF16),
        pltpu.VMEM((2, 128, C), BF16),
        pltpu.VMEM((128, C), BF16),
        pltpu.VMEM((3 * BC, C), F32),
        pltpu.VMEM((3 * BC, C), F32),
        pltpu.VMEM((2, 128, C), F32),
        pltpu.VMEM((2, 128, C), F32),
        pltpu.VMEM((2, 128, C), F32),
        pltpu.VMEM((128, C), F32),
        pltpu.VMEM((128, C), F32),
        pltpu.VMEM((2, HEADS * NB, 2 * NB), F32),
        pltpu.VMEM((2, HEADS * 2 * NC, 4 * NC), F32),
        pltpu.VMEM((16, 128), F32),
        pltpu.VMEM((3 * BC, C), F32),
        pltpu.VMEM((128, C), F32),
        pltpu.VMEM((2, 128, C), BF16),
        pltpu.VMEM((2, 3 * BC, C), BF16),
        pltpu.VMEM((6 * NC, C), BF16),
        pltpu.SemaphoreType.DMA((7,)),
        pltpu.SemaphoreType.DMA((8,)),
        pltpu.SemaphoreType.DMA((8,)),
        pltpu.SemaphoreType.REGULAR,
    ]
    return pl.pallas_call(
        functools.partial(kernel, n_lat, n_lon),
        out_shape=pltpu.VMEM((6, 12, 12, C), BF16),
        in_specs=[pl.BlockSpec(memory_space=pltpu.HBM)] * 7,
        out_specs=pl.BlockSpec(memory_space=pltpu.VMEM),
        scratch_shapes=scratch,
        compiler_params=pltpu.CompilerParams(
            collective_id=0, has_side_effects=True, vmem_limit_bytes=40 * 1024 * 1024
        ),
    )(*args)


def solution(mesh):
    placed = (
        P(None, "lat", "lon", None),
        P("lat", None, None, None),
        P("lat", "lon"),
        P(),
        P(),
        P(),
        P(),
    )
    return jax.shard_map(
        functools.partial(shards, mesh.shape["lat"], mesh.shape["lon"]),
        mesh=mesh,
        in_specs=placed,
        out_specs=P(None, "lat", "lon", None),
        check_vma=False,
    )
```

```python
import functools

import jax
import jax.numpy as jnp
from jax import lax
from jax.experimental import pallas as pl
from jax.experimental.pallas import tpu as pltpu
from jax.sharding import PartitionSpec as P

HEADS = 6
C = 192
FF = 768
HALF = 6
NB = 72
NC = 40
BC = NB + NC
EPS = 1e-05
NEG = -1000000000.0
SCALE = 1.0 / 32**0.5
MESH = pl.DeviceIdType.MESH
F32 = jnp.float32
BF16 = jnp.bfloat16

FULL = (224, 112, 112)
HALVED = (128, 64, 64)


def dot(a, b):
    return jnp.dot(a, b, preferred_element_type=F32)


def dot_nt(a, b):
    return lax.dot_general(a, b, (((1,), (1,)), ((), ())), preferred_element_type=F32)


def dot_tt(a, b):
    return lax.dot_general(a, b, (((0,), (1,)), ((), ())), preferred_element_type=F32)


def dot_tn(a, b):
    return lax.dot_general(a, b, (((0,), (0,)), ((), ())), preferred_element_type=F32)


def layer_norm(values):
    average = jnp.mean(values, axis=-1, keepdims=True)
    centred = values - average
    variance = jnp.mean(centred * centred, axis=-1, keepdims=True)
    return centred * lax.rsqrt(variance + EPS)


def one_hot(hit):
    return jnp.where(hit, 1.0, 0.0).astype(BF16)


def iota(shape, axis):
    return lax.broadcasted_iota(jnp.int32, shape, axis)


def by36(t):
    return (t * 57) >> 11


def by18(t):
    return (t * 57) >> 10


def by6(t):
    return (t * 43) >> 8


def gather_of(side):
    t = iota((BC + NC, 1), 0)
    is_b = t < NB
    is_a = t >= BC
    u = jnp.where(is_a, t - BC, t - NB)
    lev = jnp.where(is_b, by36(t), by18(u))
    v = jnp.where(is_b, t - 36 * lev, u - 18 * lev)
    row = by6(v)
    col = v - 6 * row + HALF * side
    row = row + jnp.where(is_b, 3, jnp.where(is_a, 0, 9))
    source = lev * 192 + row * 16 + col
    source = jnp.where(is_b | (u < 36), source, -1)
    return one_hot(iota((BC + NC, 384), 1) == source)


def scatter_of(lev, rows, full):
    d = iota((rows * 16, 1), 0)
    row, col = d >> 4, d & 15
    side = jnp.where(col >= HALF, 1, 0)
    cc = col - HALF * side
    if full:
        at = jnp.where(row < 6, lev * 36 + row * 6 + cc, NB + lev * 18 + (row - 6) * 6 + cc)
        width = BC
    else:
        at = lev * 18 + row * 6 + cc
        width = NC
    source = jnp.where(col < 12, side * width + at, -1)
    return one_hot(iota((rows * 16, 2 * width), 1) == source)


def key_place(t, band, side):
    if band == 0:
        halo = t >= NB
        u = jnp.where(halo, t - NB, t)
        lev = by36(u)
        v = u - 36 * lev
        row = by6(v)
        col = v - 6 * row
        valid = t >= 0
    else:
        halo = t >= 2 * NC
        w = jnp.where(halo, t - 2 * NC, t)
        below = w >= NC
        u = jnp.where(below, w - NC, w)
        lev = by18(u)
        v = u - 18 * lev
        row = by6(v)
        col = v - 6 * row
        row = row + jnp.where(below, 3, 0)
        valid = u < 36
    col = col + jnp.where(halo, HALF * side, HALF * (1 - side))
    return lev, row, col, valid


def pack(buf, x, form):
    tokens, rest, second = form
    buf[0:tokens, :] = x[:, 0:128].astype(BF16)
    low, high = x[0:rest, 128:192], x[second : second + rest, 128:192]
    buf[tokens : tokens + rest, :] = jnp.concatenate([low, high], axis=1).astype(BF16)


def unpack(dst, buf, form):
    tokens, rest, second = form
    dst[0:tokens, 0:128] = buf[0:tokens, :]
    tail = buf[tokens : tokens + rest, :]
    dst[0:rest, 128:192] = tail[:, 0:64]
    dst[second : second + rest, 128:192] = tail[:, 64:128]


def attend(windows):
    n = windows[0][0].shape[0]
    head = iota((1, C), 1) >> 5
    stacked = [jnp.concatenate([jnp.where(head == h, q, 0.0) for h in range(HEADS)], axis=0).astype(BF16) for q, *_ in windows]
    scores = [dot_nt(s, k) * SCALE + bias for s, (_, k, _, bias) in zip(stacked, windows)]
    tops = [jnp.max(s, axis=-1, keepdims=True) for s in scores]
    weights = [jnp.exp(s - t) for s, t in zip(scores, tops)]
    totals = [1.0 / jnp.sum(w, axis=-1, keepdims=True) for w in weights]
    outs = []
    for w, t, (_, _, v, _) in zip(weights, totals, windows):
        mixed = dot(w.astype(BF16), v) * t
        out = jnp.where(head == 0, mixed[0:n], 0.0)
        for h in range(1, HEADS):
            out = jnp.where(head == h, mixed[h * n : (h + 1) * n], out)
        outs.append(out)
    return outs


def feed_forward(residual, w_up, w_down):
    normed = layer_norm(residual).astype(BF16)
    hidden = jax.nn.gelu(dot(normed, w_up)).astype(BF16)
    return residual + dot(hidden, w_down)


def kernel(
    n_lat,
    n_lon,
    state,
    attn_bias,
    region_ids,
    w_qkv,
    w_out,
    w_up,
    w_down,
    out,
    x_in,
    bias_in,
    region,
    region_left,
    wqkv_v,
    wq,
    wk,
    wv,
    wo_v,
    wu_v,
    wd_v,
    wd_t,
    xp,
    st,
    normed_b,
    normed_c,
    normed_a,
    m_b,
    m_c,
    m_lat,
    m_ret,
    r_b,
    r_c,
    r_lat,
    r_diag,
    r_ret,
    own_b,
    own_c,
    halo_bx,
    halo_cx,
    lat_x,
    diag_x,
    halo_b,
    halo_c,
    lat_q,
    lat_k,
    lat_v,
    diag_k,
    diag_v,
    bias_b,
    bias_c,
    labels,
    mix,
    mix_ret,
    ret_x,
    out_bc,
    out_a,
    load_sem,
    send_sem,
    recv_sem,
    here_sem,
):
    la = lax.axis_index("lat")
    lo = lax.axis_index("lon")
    right = lax.rem(lo + 1, n_lon)
    left = lax.rem(lo + n_lon - 1, n_lon)
    has_above = la > 0
    has_below = la < n_lat - 1
    half = n_lon // 2
    far_left = lax.rem(lo, half) == 0
    far_right = lax.rem(lo + 1, half) == 0
    end = far_left | far_right
    end_on_left = lax.rem(lo + half - 1, half) == 0
    end_on_right = lax.rem(lo + 2, half) == 0
    mate = end_on_left | end_on_right
    near = jnp.where(far_left, right, jnp.where(far_right, left, lo))
    sides = ((far_left, left), (far_right, right))

    barrier = pltpu.get_barrier_semaphore()

    def greet(row, col):
        pl.semaphore_signal(barrier, inc=1, device_id=(row, col), device_id_type=MESH)

    pl.when(jnp.logical_not(end_on_left))(functools.partial(greet, la, left))
    pl.when(jnp.logical_not(end_on_right))(functools.partial(greet, la, right))
    for there, row in ((has_above, la - 1), (has_below, la + 1)):
        pl.when(there)(functools.partial(greet, row, near))
        for far, col in sides:
            pl.when(there & far)(functools.partial(greet, row, col))

    loads = [
        pltpu.make_async_copy(src, dst, load_sem.at[i])
        for i, (src, dst) in enumerate(
            [
                (state, x_in),
                (w_qkv, wqkv_v),
                (attn_bias, bias_in),
                (region_ids, region),
                (w_out, wo_v),
                (w_up, wu_v),
                (w_down, wd_v),
            ]
        )
    ]
    for load in loads:
        load.start()

    xp[...] = jnp.zeros_like(xp)
    for ref in (normed_a, normed_b, normed_c):
        ref[...] = jnp.zeros_like(ref)
    mix_ret[...] = jnp.zeros_like(mix_ret)
    gathers = [gather_of(0), gather_of(1)]
    loads[0].wait()
    for lev in range(6):
        xp[lev, :, 0:12, :] = x_in[(lev + 1) % 6].astype(F32)
    for z in range(3):
        tokens = xp[2 * z : 2 * z + 2].reshape(384, C).astype(BF16)
        for side in range(2):
            x = dot(gathers[side], tokens)
            st[side, z] = x
            x = layer_norm(x)
            normed_b[side, z * NB : (z + 1) * NB, :] = x[0:NB]
            normed_c[side, z * NC : (z + 1) * NC, :] = x[NB:BC]
            normed_a[side, z * NC : (z + 1) * NC, :] = x[BC : BC + NC]
    for side in range(2):
        pack(m_b.at[side], normed_b[side], FULL)
        pack(m_c.at[side], normed_c[side], HALVED)
        pack(m_lat.at[side], normed_a[side], HALVED)

    def remote(src, dst, i, device):
        return pltpu.make_async_remote_copy(
            src_ref=src,
            dst_ref=dst,
            send_sem=send_sem.at[i],
            recv_sem=recv_sem.at[i],
            device_id=device,
            device_id_type=MESH,
        )

    def along_b(side, col):
        return remote(m_b.at[side], r_b.at[1 - side], 1 - side, (la, col))

    def along_c(side, col):
        return remote(m_c.at[side], r_c.at[1 - side], 9 - side, (la, col))

    def corner(side, source, row, col):
        return remote(source.at[side], r_diag.at[1 - side], 3 - side, (row, col))

    regions = remote(region_ids, region_left, 4, (la, right))
    up = remote(m_lat, r_lat, 5, (la - 1, lo))

    rows = jnp.where(has_above, 1, 0) + jnp.where(has_below, 1, 0)

    def send_near():
        @pl.when(jnp.logical_not(end))
        def _():
            pl.semaphore_wait(barrier, 2 + rows * jnp.where(mate, 2, 1))

        @pl.when(mate)
        def _():
            col = jnp.where(end_on_left, left, right)
            pl.semaphore_signal(here_sem, inc=1, device_id=(la, col), device_id_type=MESH)

        @pl.when(end)
        def _():
            pl.semaphore_wait(here_sem, 1)

        pl.when(has_above)(up.start)
        pl.when(jnp.logical_not(far_right))(regions.start)
        for side, (far, col) in enumerate(sides):
            pl.when(jnp.logical_not(far))(along_b(side, col).start)
            pl.when(jnp.logical_not(far))(along_c(side, col).start)

    def send_far():
        pl.semaphore_wait(barrier, 1 + rows)
        pl.when(far_right)(regions.start)
        for side, (far, col) in enumerate(sides):
            pl.when(far & has_above)(corner(side, m_lat, la - 1, col).start)
            pl.when(far)(along_c(side, col).start)
            pl.when(far)(along_b(side, col).start)

    def prepare():
        loads[1].wait()
        wq[...] = wqkv_v[:, 0:192]
        wk[...] = wqkv_v[:, 192:384]
        wv[...] = wqkv_v[:, 384:576]
        for side in range(2):
            for own, normed in ((own_b, normed_b), (own_c, normed_c)):
                x = normed[side].astype(BF16)
                for i, w in enumerate((wq, wk, wv)):
                    own[side, i] = dot(x, w[...])
        loads[2].wait()
        for band, (store, n, m) in enumerate(((bias_b, NB, 2 * NB), (bias_c, 2 * NC, 4 * NC))):
            for side in range(2):
                lev, row, col, valid = key_place(iota((m, 1), 0), band, side)
                at = jnp.where(valid, lev * 72 + row * 12 + col, -1)
                select = one_hot(iota((m, 144), 1) == at)
                rows = [dot(select[0:n], bias_in[band, h]) for h in range(HEADS)]
                rows = jnp.concatenate(rows, axis=0).astype(BF16)
                store[side] = dot_nt(rows, select)
        loads[3].wait()
        apply_mask(1, region)
        loads[6].wait()
        wd_t[...] = wd_v[...].T

    def apply_mask(side, source):
        labels[...] = jnp.zeros_like(labels)
        labels[0:12, 0:12] = source[...].astype(F32)
        table = labels[...].astype(BF16)
        for band, (store, n, m) in enumerate(((bias_b, NB, 2 * NB), (bias_c, 2 * NC, 4 * NC))):
            _, row, col, _ = key_place(iota((m, 1), 0), band, side)
            in_row = one_hot(iota((m, 16), 1) == row + 6 * band)
            queries = dot(in_row[0:n], table)
            queries = jnp.where(iota((n, 128), 1) == col[0:n], queries, 0.0)
            queries = jnp.sum(queries, axis=1, keepdims=True)
            _, row, col, valid = key_place(iota((1, m), 1), band, side)
            keys = dot_tt(table, in_row)
            keys = jnp.where(iota((128, m), 0) == col, keys, 0.0)
            keys = jnp.sum(keys, axis=0, keepdims=True)
            valid = valid & (la * 12 + 6 * band + row < n_lat * 12 - 3)
            keys = jnp.where(valid, keys, -1.0)
            allowed = queries == keys
            for h in range(HEADS):
                part = store[side, h * n : (h + 1) * n, :]
                store[side, h * n : (h + 1) * n, :] = jnp.where(allowed, part, NEG)

    def start(i, carry):
        far_first = lo >= half
        pl.when(i == jnp.where(far_first, 1, 0))(send_near)
        pl.when(end & (i == jnp.where(far_first, 0, 2)))(send_far)
        pl.when(i == jnp.where(far_first, 2, 1))(prepare)
        return carry

    lax.fori_loop(0, 3, start, 0)

    loads[4].wait()
    loads[5].wait()

    def down(side):
        return remote(m_ret.at[side], r_ret.at[side], 6 + side, (la + 1, lo))

    def mask(side):
        @pl.when(side == 0)
        def _():
            regions.wait_recv()
            apply_mask(0, region_left)

    def halo(copy, x_ref, buf, keys_values, form):
        copy.wait_recv()
        unpack(x_ref, buf, form)
        x = x_ref[...]
        keys_values[0] = dot(x, wk[...])
        keys_values[1] = dot(x, wv[...])

    def rows_below():
        @pl.when(has_below)
        def _():
            up.wait_recv()
            for side, (far, col) in enumerate(sides):
                pl.when(jnp.logical_not(far))(corner(side, r_lat, la, col).start)

        @pl.when(jnp.logical_not(has_below))
        def _():
            r_lat[...] = jnp.zeros_like(r_lat)
            r_diag[...] = jnp.zeros_like(r_diag)

        for side in range(2):
            unpack(lat_x.at[side], r_lat.at[side], HALVED)
            x = lat_x[side]
            lat_q[side] = dot(x, wq[...])
            lat_k[side] = dot(x, wk[...])
            lat_v[side] = dot(x, wv[...])

    def windows_c(side):
        @pl.when(has_below)
        def _():
            corner(1 - side, r_lat, la, left).wait_recv()

        halo(along_c(1 - side, left), halo_cx, r_c.at[side], halo_c, HALVED)
        unpack(diag_x, r_diag.at[side], HALVED)
        x = diag_x[...]
        diag_k[...] = dot(x, wk[...])
        diag_v[...] = dot(x, wv[...])
        windows = []
        for z in range(3):
            a = pl.ds(z * NC, NC)
            q = jnp.concatenate([own_c[side, 0, a], lat_q[side, a]], axis=0)
            k = jnp.concatenate([own_c[side, 1, a], lat_k[side, a], halo_c[0, a], diag_k[a]], axis=0)
            v = jnp.concatenate([own_c[side, 2, a], lat_v[side, a], halo_c[1, a], diag_v[a]], axis=0)
            windows.append((q, k.astype(BF16), v.astype(BF16), bias_c[side]))
        context = jnp.concatenate(attend(windows), axis=0)
        mixed = dot(context.astype(BF16), wo_v[...]).astype(BF16).astype(F32)
        for z in range(3):
            at = z * 2 * NC
            mix[side, z * BC + NB : (z + 1) * BC, :] = mixed[at : at + NC]
            mix_ret[z * NC : (z + 1) * NC, :] = mixed[at + NC : at + 2 * NC]
        pack(m_ret.at[side], mix_ret[...], HALVED)

        @pl.when(has_below)
        def _():
            down(side).start()

    def windows_b(side):
        halo(along_b(1 - side, left), halo_bx, r_b.at[side], halo_b, FULL)
        windows = []
        for z in range(3):
            b = pl.ds(z * NB, NB)
            k = jnp.concatenate([own_b[side, 1, b], halo_b[0, b]], axis=0)
            v = jnp.concatenate([own_b[side, 2, b], halo_b[1, b]], axis=0)
            windows.append((own_b[side, 0, b], k.astype(BF16), v.astype(BF16), bias_b[side]))
        context = jnp.concatenate(attend(windows), axis=0)
        mixed = dot(context.astype(BF16), wo_v[...]).astype(BF16).astype(F32)
        for z in range(3):
            mix[side, z * BC : z * BC + NB, :] = mixed[z * NB : (z + 1) * NB]

    def feed(side):
        residual = jnp.concatenate([st[side, z, 0:BC] for z in range(3)], axis=0) + mix[side]
        out_bc[side] = feed_forward(residual, wu_v[...], wd_t[...]).astype(BF16)

    late = lax.rem(la, 4) == 3
    first_right = far_left | end_on_left

    def task(step, carry):
        second = (step >= 3) & (step != 4) | jnp.where(late, step == 2, step == 4)
        second = jnp.where(second, 1, 0)
        side = jnp.where(first_right, 1 - second, second)
        second_c = jnp.where(late, 2, 3)
        pl.when((step == 0) | (step == second_c))(functools.partial(mask, side))
        pl.when(step == 1)(rows_below)
        pl.when((step == 1) | (step == second_c))(functools.partial(windows_c, side))
        pl.when((step == 0) | (step == second_c + 1))(functools.partial(windows_b, side))
        pl.when((step == 5) | (step == jnp.where(late, 4, 2)))(functools.partial(feed, side))
        return carry

    lax.fori_loop(0, 6, task, 0)

    for lev in range(2):
        scatter = scatter_of(lev, 9, True)
        for z in range(3):
            part = pl.ds(z * BC, BC)
            grid = dot(scatter, jnp.concatenate([out_bc[0, part], out_bc[1, part]], axis=0)).reshape(9, 16, C)
            out[(2 * z + lev + 1) % 6, 3:12] = grid[:, 0:12, :].astype(BF16)

    @pl.when(has_above)
    def _():
        down(0).wait_recv()
        down(1).wait_recv()

    @pl.when(jnp.logical_not(has_above))
    def _():
        r_ret[...] = jnp.zeros_like(r_ret)

    for side in range(2):
        unpack(ret_x.at[side], r_ret.at[side], HALVED)
    residual = [
        st[side, z, BC : BC + NC] + ret_x[side, z * NC : (z + 1) * NC, :].astype(F32) for z in range(3) for side in range(2)
    ]
    out_a[...] = feed_forward(jnp.concatenate(residual, axis=0), wu_v[...], wd_t[...]).astype(BF16)
    for lev in range(2):
        scatter = scatter_of(lev, 3, False)
        for z in range(3):
            grid = dot(scatter, out_a[z * 2 * NC : (z + 1) * 2 * NC, :]).reshape(3, 16, C)
            out[(2 * z + lev + 1) % 6, 0:3] = grid[:, 0:12, :].astype(BF16)

    for copy in (along_b, along_c):
        copy(0, left).wait_send()
        copy(1, right).wait_send()
    regions.wait_send()

    @pl.when(has_above)
    def _():
        for side, (far, col) in enumerate(sides):
            pl.when(far)(corner(side, m_lat, la - 1, col).wait_send)
        up.wait_send()

    @pl.when(has_below)
    def _():
        for side, (far, col) in enumerate(sides):
            pl.when(jnp.logical_not(far))(corner(side, r_lat, la, col).wait_send)
        down(0).wait_send()
        down(1).wait_send()


def shards(n_lat, n_lon, *args):
    args = (*args[:6], args[6].T)
    args = [pltpu.with_memory_space_constraint(a, pltpu.HBM) for a in args]
    def packed(form, *lead):
        return pltpu.VMEM((*lead, form[0] + form[1], 128), BF16)

    scratch = [
        pltpu.VMEM((6, 12, 12, C), BF16),
        pltpu.VMEM((2, HEADS, 144, 144), BF16),
        pltpu.VMEM((12, 12), jnp.int32),
        pltpu.VMEM((12, 12), jnp.int32),
        pltpu.VMEM((C, 3 * C), BF16),
        pltpu.VMEM((C, C), BF16),
        pltpu.VMEM((C, C), BF16),
        pltpu.VMEM((C, C), BF16),
        pltpu.VMEM((C, C), BF16),
        pltpu.VMEM((C, FF), BF16),
        pltpu.VMEM((C, FF), BF16),
        pltpu.VMEM((FF, C), BF16),
        pltpu.VMEM((6, 12, 16, C), F32),
        pltpu.VMEM((2, 3, BC + NC, C), F32),
        pltpu.VMEM((2, 224, C), F32),
        pltpu.VMEM((2, 128, C), F32),
        pltpu.VMEM((2, 128, C), F32),
        packed(FULL, 2),
        packed(HALVED, 2),
        packed(HALVED, 2),
        packed(HALVED, 2),
        packed(FULL, 2),
        packed(HALVED, 2),
        packed(HALVED, 2),
        packed(HALVED, 2),
        packed(HALVED, 2),
        pltpu.VMEM((2, 3, 224, C), F32),
        pltpu.VMEM((2, 3, 128, C), F32),
        pltpu.VMEM((224, C), BF16),
        pltpu.VMEM((128, C), BF16),
        pltpu.VMEM((2, 128, C), BF16),
        pltpu.VMEM((128, C), BF16),
        pltpu.VMEM((2, 224, C), F32),
        pltpu.VMEM((2, 128, C), F32),
        pltpu.VMEM((2, 128, C), F32),
        pltpu.VMEM((2, 128, C), F32),
        pltpu.VMEM((2, 128, C), F32),
        pltpu.VMEM((128, C), F32),
        pltpu.VMEM((128, C), F32),
        pltpu.VMEM((2, HEADS * NB, 2 * NB), F32),
        pltpu.VMEM((2, HEADS * 2 * NC, 4 * NC), F32),
        pltpu.VMEM((16, 128), F32),
        pltpu.VMEM((2, 3 * BC, C), F32),
        pltpu.VMEM((128, C), F32),
        pltpu.VMEM((2, 128, C), BF16),
        pltpu.VMEM((2, 3 * BC, C), BF16),
        pltpu.VMEM((6 * NC, C), BF16),
        pltpu.SemaphoreType.DMA((7,)),
        pltpu.SemaphoreType.DMA((10,)),
        pltpu.SemaphoreType.DMA((10,)),
        pltpu.SemaphoreType.REGULAR,
    ]
    return pl.pallas_call(
        functools.partial(kernel, n_lat, n_lon),
        out_shape=pltpu.VMEM((6, 12, 12, C), BF16),
        in_specs=[pl.BlockSpec(memory_space=pltpu.HBM)] * 7,
        out_specs=pl.BlockSpec(memory_space=pltpu.VMEM),
        scratch_shapes=scratch,
        compiler_params=pltpu.CompilerParams(
            collective_id=0, has_side_effects=True, vmem_limit_bytes=40 * 1024 * 1024
        ),
    )(*args)


def solution(mesh):
    placed = (
        P(None, "lat", "lon", None),
        P("lat", None, None, None),
        P("lat", "lon"),
        P(),
        P(),
        P(),
        P(),
    )
    return jax.shard_map(
        functools.partial(shards, mesh.shape["lat"], mesh.shape["lon"]),
        mesh=mesh,
        in_specs=placed,
        out_specs=P(None, "lat", "lon", None),
        check_vma=False,
    )
```

```python
import functools

import jax
import jax.numpy as jnp
from jax import lax
from jax.experimental import pallas as pl
from jax.experimental.pallas import tpu as pltpu
from jax.sharding import PartitionSpec as P

HEADS = 6
C = 192
FF = 768
HALF = 6
NB = 72
NC = 40
BC = NB + NC
EPS = 1e-05
NEG = -1000000000.0
SCALE = 1.0 / 32**0.5
MESH = pl.DeviceIdType.MESH
F32 = jnp.float32
BF16 = jnp.bfloat16

FULL = (224, 112, 112)
HALVED = (128, 64, 64)


def dot(a, b):
    return jnp.dot(a, b, preferred_element_type=F32)


def dot_nt(a, b):
    return lax.dot_general(a, b, (((1,), (1,)), ((), ())), preferred_element_type=F32)


def dot_tt(a, b):
    return lax.dot_general(a, b, (((0,), (1,)), ((), ())), preferred_element_type=F32)


def dot_tn(a, b):
    return lax.dot_general(a, b, (((0,), (0,)), ((), ())), preferred_element_type=F32)


def layer_norm(values):
    average = jnp.mean(values, axis=-1, keepdims=True)
    centred = values - average
    variance = jnp.mean(centred * centred, axis=-1, keepdims=True)
    return centred * lax.rsqrt(variance + EPS)


def one_hot(hit):
    return jnp.where(hit, 1.0, 0.0).astype(BF16)


def iota(shape, axis):
    return lax.broadcasted_iota(jnp.int32, shape, axis)


def by36(t):
    return (t * 57) >> 11


def by18(t):
    return (t * 57) >> 10


def by6(t):
    return (t * 43) >> 8


def gather_of(side):
    t = iota((BC + NC, 1), 0)
    is_b = t < NB
    is_a = t >= BC
    u = jnp.where(is_a, t - BC, t - NB)
    lev = jnp.where(is_b, by36(t), by18(u))
    v = jnp.where(is_b, t - 36 * lev, u - 18 * lev)
    row = by6(v)
    col = v - 6 * row + HALF * side
    row = row + jnp.where(is_b, 3, jnp.where(is_a, 0, 9))
    source = lev * 192 + row * 16 + col
    source = jnp.where(is_b | (u < 36), source, -1)
    return one_hot(iota((BC + NC, 384), 1) == source)


def scatter_of(lev, full):
    rows, width = (6, NB) if full else (3, NC)
    d = iota((rows * 16, 1), 0)
    row, col = d >> 4, d & 15
    side = jnp.where(col >= HALF, 1, 0)
    source = side * width + lev * rows * HALF + row * HALF + col - HALF * side
    source = jnp.where(col < 12, source, -1)
    return one_hot(iota((rows * 16, 2 * width), 1) == source)


def key_place(t, band, side):
    if band == 0:
        halo = t >= NB
        u = jnp.where(halo, t - NB, t)
        lev = by36(u)
        v = u - 36 * lev
        row = by6(v)
        col = v - 6 * row
        valid = t >= 0
    else:
        halo = t >= 2 * NC
        w = jnp.where(halo, t - 2 * NC, t)
        below = w >= NC
        u = jnp.where(below, w - NC, w)
        lev = by18(u)
        v = u - 18 * lev
        row = by6(v)
        col = v - 6 * row
        row = row + jnp.where(below, 3, 0)
        valid = u < 36
    col = col + jnp.where(halo, HALF * side, HALF * (1 - side))
    return lev, row, col, valid


def pack(buf, x, form):
    tokens, rest, second = form
    buf[0:tokens, :] = x[:, 0:128].astype(BF16)
    low, high = x[0:rest, 128:192], x[second : second + rest, 128:192]
    buf[tokens : tokens + rest, :] = jnp.concatenate([low, high], axis=1).astype(BF16)


def unpack(dst, buf, form):
    tokens, rest, second = form
    dst[0:tokens, 0:128] = buf[0:tokens, :]
    tail = buf[tokens : tokens + rest, :]
    dst[0:rest, 128:192] = tail[:, 0:64]
    dst[second : second + rest, 128:192] = tail[:, 64:128]


def attend(windows):
    n = windows[0][0].shape[0]
    head = iota((1, C), 1) >> 5
    stacked = [jnp.concatenate([jnp.where(head == h, q, 0.0) for h in range(HEADS)], axis=0).astype(BF16) for q, *_ in windows]
    scores = [dot_nt(s, k) * SCALE + bias for s, (_, k, _, bias) in zip(stacked, windows)]
    tops = [jnp.max(s, axis=-1, keepdims=True) for s in scores]
    weights = [jnp.exp(s - t) for s, t in zip(scores, tops)]
    totals = [1.0 / jnp.sum(w, axis=-1, keepdims=True) for w in weights]
    outs = []
    for w, t, (_, _, v, _) in zip(weights, totals, windows):
        mixed = dot(w.astype(BF16), v) * t
        out = jnp.where(head == 0, mixed[0:n], 0.0)
        for h in range(1, HEADS):
            out = jnp.where(head == h, mixed[h * n : (h + 1) * n], out)
        outs.append(out)
    return outs


def feed_forward(residual, w_up, w_down):
    normed = layer_norm(residual).astype(BF16)
    hidden = jax.nn.gelu(dot(normed, w_up)).astype(BF16)
    return residual + dot(hidden, w_down)


def kernel(
    n_lat,
    n_lon,
    state,
    attn_bias,
    region_ids,
    w_qkv,
    w_out,
    w_up,
    w_down,
    out,
    x_in,
    bias_in,
    region,
    region_left,
    wqkv_v,
    wq,
    wk,
    wv,
    wo_v,
    wu_v,
    wd_v,
    wd_t,
    xp,
    st,
    normed_b,
    normed_c,
    normed_a,
    m_b,
    m_c,
    m_lat,
    m_ret,
    r_b,
    r_c,
    r_lat,
    r_diag,
    r_ret,
    own_b,
    own_c,
    halo_bx,
    halo_cx,
    lat_x,
    diag_x,
    halo_b,
    halo_c,
    lat_q,
    lat_k,
    lat_v,
    diag_k,
    diag_v,
    bias_b,
    bias_c,
    labels,
    mix_b,
    mix_c,
    mix_ret,
    ret_x,
    out_b,
    load_sem,
    send_sem,
    recv_sem,
    here_sem,
):
    la = lax.axis_index("lat")
    lo = lax.axis_index("lon")
    right = lax.rem(lo + 1, n_lon)
    left = lax.rem(lo + n_lon - 1, n_lon)
    has_above = la > 0
    has_below = la < n_lat - 1
    half = n_lon // 2
    far_left = lax.rem(lo, half) == 0
    far_right = lax.rem(lo + 1, half) == 0
    end = far_left | far_right
    end_on_left = lax.rem(lo + half - 1, half) == 0
    end_on_right = lax.rem(lo + 2, half) == 0
    mate = end_on_left | end_on_right
    near = jnp.where(far_left, right, jnp.where(far_right, left, lo))
    sides = ((far_left, left), (far_right, right))

    barrier = pltpu.get_barrier_semaphore()

    def greet(row, col):
        pl.semaphore_signal(barrier, inc=1, device_id=(row, col), device_id_type=MESH)

    pl.when(jnp.logical_not(end_on_left))(functools.partial(greet, la, left))
    pl.when(jnp.logical_not(end_on_right))(functools.partial(greet, la, right))
    for there, row in ((has_above, la - 1), (has_below, la + 1)):
        pl.when(there)(functools.partial(greet, row, near))
        for far, col in sides:
            pl.when(there & far)(functools.partial(greet, row, col))

    loads = [
        pltpu.make_async_copy(src, dst, load_sem.at[i])
        for i, (src, dst) in enumerate(
            [
                (state, x_in),
                (w_qkv, wqkv_v),
                (attn_bias, bias_in),
                (region_ids, region),
                (w_out, wo_v),
                (w_up, wu_v),
                (w_down, wd_v),
            ]
        )
    ]
    for load in loads:
        load.start()

    xp[...] = jnp.zeros_like(xp)
    for ref in (normed_a, normed_b, normed_c):
        ref[...] = jnp.zeros_like(ref)
    mix_ret[...] = jnp.zeros_like(mix_ret)
    gathers = [gather_of(0), gather_of(1)]
    loads[0].wait()
    for lev in range(6):
        xp[lev, :, 0:12, :] = x_in[(lev + 1) % 6].astype(F32)
    for z in range(3):
        tokens = xp[2 * z : 2 * z + 2].reshape(384, C).astype(BF16)
        for side in range(2):
            x = dot(gathers[side], tokens)
            st[side, z] = x
            x = layer_norm(x)
            normed_b[side, z * NB : (z + 1) * NB, :] = x[0:NB]
            normed_c[side, z * NC : (z + 1) * NC, :] = x[NB:BC]
            normed_a[side, z * NC : (z + 1) * NC, :] = x[BC : BC + NC]
    for side in range(2):
        pack(m_b.at[side], normed_b[side], FULL)
        pack(m_c.at[side], normed_c[side], HALVED)
        pack(m_lat.at[side], normed_a[side], HALVED)

    def remote(src, dst, i, device):
        return pltpu.make_async_remote_copy(
            src_ref=src,
            dst_ref=dst,
            send_sem=send_sem.at[i],
            recv_sem=recv_sem.at[i],
            device_id=device,
            device_id_type=MESH,
        )

    def along_b(side, col):
        return remote(m_b.at[side], r_b.at[1 - side], 1 - side, (la, col))

    def along_c(side, col):
        return remote(m_c.at[side], r_c.at[1 - side], 9 - side, (la, col))

    def corner(side, source, row, col):
        return remote(source.at[side], r_diag.at[1 - side], 3 - side, (row, col))

    regions = remote(region_ids, region_left, 4, (la, right))
    up = remote(m_lat, r_lat, 5, (la - 1, lo))

    rows = jnp.where(has_above, 1, 0) + jnp.where(has_below, 1, 0)

    def send_near():
        @pl.when(jnp.logical_not(end))
        def _():
            pl.semaphore_wait(barrier, 2 + rows * jnp.where(mate, 2, 1))

        @pl.when(mate)
        def _():
            col = jnp.where(end_on_left, left, right)
            pl.semaphore_signal(here_sem, inc=1, device_id=(la, col), device_id_type=MESH)

        @pl.when(end)
        def _():
            pl.semaphore_wait(here_sem, 1)

        pl.when(has_above)(up.start)
        pl.when(jnp.logical_not(far_right))(regions.start)
        for side, (far, col) in enumerate(sides):
            pl.when(jnp.logical_not(far))(along_b(side, col).start)
            pl.when(jnp.logical_not(far))(along_c(side, col).start)

    def send_far():
        pl.semaphore_wait(barrier, 1 + rows)
        pl.when(far_right)(regions.start)
        for side, (far, col) in enumerate(sides):
            pl.when(far & has_above)(corner(side, m_lat, la - 1, col).start)
            pl.when(far)(along_c(side, col).start)
            pl.when(far)(along_b(side, col).start)

    def prepare():
        loads[1].wait()
        wq[...] = wqkv_v[:, 0:192]
        wk[...] = wqkv_v[:, 192:384]
        wv[...] = wqkv_v[:, 384:576]
        for side in range(2):
            for own, normed in ((own_b, normed_b), (own_c, normed_c)):
                x = normed[side].astype(BF16)
                for i, w in enumerate((wq, wk, wv)):
                    own[side, i] = dot(x, w[...])
        loads[2].wait()
        for band, (store, n, m) in enumerate(((bias_b, NB, 2 * NB), (bias_c, 2 * NC, 4 * NC))):
            for side in range(2):
                lev, row, col, valid = key_place(iota((n, 1), 0), band, side)
                at = jnp.where(valid, lev * 72 + row * 12 + col, -1)
                select = one_hot(iota((n, 144), 1) == at)
                rows = [dot(select, bias_in[band, h]) for h in range(HEADS)]
                rows = jnp.concatenate(rows, axis=0).astype(BF16)
                lev, row, col, valid = key_place(iota((1, m), 1), band, side)
                at = jnp.where(valid, lev * 72 + row * 12 + col, -1)
                store[side] = dot(rows, one_hot(iota((144, m), 0) == at))
        loads[3].wait()
        apply_mask(1, region)
        loads[6].wait()
        wd_t[...] = wd_v[...].T

    def apply_mask(side, source):
        labels[...] = jnp.zeros_like(labels)
        labels[0:12, 0:12] = source[...].astype(F32)
        table = labels[...].astype(BF16)
        for band, (store, n, m) in enumerate(((bias_b, NB, 2 * NB), (bias_c, 2 * NC, 4 * NC))):
            _, row, col, _ = key_place(iota((m, 1), 0), band, side)
            in_row = one_hot(iota((m, 16), 1) == row + 6 * band)
            queries = dot(in_row[0:n], table)
            queries = jnp.where(iota((n, 128), 1) == col[0:n], queries, 0.0)
            queries = jnp.sum(queries, axis=1, keepdims=True)
            _, row, col, valid = key_place(iota((1, m), 1), band, side)
            keys = dot_tt(table, in_row)
            keys = jnp.where(iota((128, m), 0) == col, keys, 0.0)
            keys = jnp.sum(keys, axis=0, keepdims=True)
            valid = valid & (la * 12 + 6 * band + row < n_lat * 12 - 3)
            keys = jnp.where(valid, keys, -1.0)
            allowed = queries == keys
            for h in range(HEADS):
                part = store[side, h * n : (h + 1) * n, :]
                store[side, h * n : (h + 1) * n, :] = jnp.where(allowed, part, NEG)

    def start(i, carry):
        far_first = lo >= half
        pl.when(i == jnp.where(far_first, 1, 0))(send_near)
        pl.when(end & (i == jnp.where(far_first, 0, 2)))(send_far)
        pl.when(i == jnp.where(far_first, 2, 1))(prepare)
        return carry

    lax.fori_loop(0, 3, start, 0)

    loads[4].wait()
    loads[5].wait()

    def down(side):
        return remote(m_ret.at[side], r_ret.at[side], 6 + side, (la + 1, lo))

    def mask():
        regions.wait_recv()
        apply_mask(0, region_left)

    def halo(copy, x_ref, buf, keys_values, form):
        copy.wait_recv()
        unpack(x_ref, buf, form)
        x = x_ref[...]
        keys_values[0] = dot(x, wk[...])
        keys_values[1] = dot(x, wv[...])

    def rows_below():
        @pl.when(has_below)
        def _():
            up.wait_recv()
            for side, (far, col) in enumerate(sides):
                pl.when(jnp.logical_not(far))(corner(side, r_lat, la, col).start)

        @pl.when(jnp.logical_not(has_below))
        def _():
            r_lat[...] = jnp.zeros_like(r_lat)
            r_diag[...] = jnp.zeros_like(r_diag)

        for side in range(2):
            unpack(lat_x.at[side], r_lat.at[side], HALVED)
            x = lat_x[side]
            lat_q[side] = dot(x, wq[...])
            lat_k[side] = dot(x, wk[...])
            lat_v[side] = dot(x, wv[...])

    def windows_c(side):
        @pl.when(has_below)
        def _():
            corner(1 - side, r_lat, la, left).wait_recv()

        halo(along_c(1 - side, left), halo_cx, r_c.at[side], halo_c, HALVED)
        unpack(diag_x, r_diag.at[side], HALVED)
        x = diag_x[...]
        diag_k[...] = dot(x, wk[...])
        diag_v[...] = dot(x, wv[...])
        windows = []
        for z in range(3):
            a = pl.ds(z * NC, NC)
            q = jnp.concatenate([own_c[side, 0, a], lat_q[side, a]], axis=0)
            k = jnp.concatenate([own_c[side, 1, a], lat_k[side, a], halo_c[0, a], diag_k[a]], axis=0)
            v = jnp.concatenate([own_c[side, 2, a], lat_v[side, a], halo_c[1, a], diag_v[a]], axis=0)
            windows.append((q, k.astype(BF16), v.astype(BF16), bias_c[side]))
        context = jnp.concatenate(attend(windows), axis=0)
        mixed = dot(context.astype(BF16), wo_v[...]).astype(BF16).astype(F32)
        for z in range(3):
            at = z * 2 * NC
            mix_c[side, z * NC : (z + 1) * NC, :] = mixed[at : at + NC]
            mix_ret[z * NC : (z + 1) * NC, :] = mixed[at + NC : at + 2 * NC]
        pack(m_ret.at[side], mix_ret[...], HALVED)

        @pl.when(has_below)
        def _():
            down(side).start()

    def windows_b(side):
        halo(along_b(1 - side, left), halo_bx, r_b.at[side], halo_b, FULL)
        windows = []
        for z in range(3):
            b = pl.ds(z * NB, NB)
            k = jnp.concatenate([own_b[side, 1, b], halo_b[0, b]], axis=0)
            v = jnp.concatenate([own_b[side, 2, b], halo_b[1, b]], axis=0)
            windows.append((own_b[side, 0, b], k.astype(BF16), v.astype(BF16), bias_b[side]))
        context = jnp.concatenate(attend(windows), axis=0)
        mixed = dot(context.astype(BF16), wo_v[...]).astype(BF16).astype(F32)
        for z in range(3):
            mix_b[side, z * NB : (z + 1) * NB, :] = mixed[z * NB : (z + 1) * NB]

    def feed_b(side):
        residual = jnp.concatenate([st[side, z, 0:NB] for z in range(3)], axis=0) + mix_b[side]
        out_b[side] = feed_forward(residual, wu_v[...], wd_t[...])

    late = lax.rem(la, 4) == 3
    inner = late & jnp.logical_not(end)
    first_right = far_left | end_on_left
    first = jnp.where(first_right, 1, 0)
    at_c = (jnp.where(inner, 4, jnp.where(late, 2, 1)), jnp.where(inner, 5, 3))
    at_b = (0, jnp.where(inner, 1, 4))
    at_feed = jnp.where(late & end, 1, jnp.where(inner, 3, 2))

    def task(step, carry):
        second = (step == at_c[1]) | (step == at_b[1])
        side = jnp.where(second, 1 - first, first)
        pl.when(step == jnp.where(first_right, jnp.where(inner, 1, 2), 0))(mask)
        pl.when(step == jnp.where(late, at_c[0], 0))(rows_below)
        pl.when((step == at_c[0]) | (step == at_c[1]))(functools.partial(windows_c, side))
        pl.when((step == at_b[0]) | (step == at_b[1]))(functools.partial(windows_b, side))
        pl.when(step == at_feed)(functools.partial(feed_b, side))
        return carry

    lax.fori_loop(0, 6, task, 0)

    def put(lev, z, row, grid):
        rows = grid.shape[0] // 16
        out[(2 * z + lev + 1) % 6, row : row + rows] = grid.reshape(rows, 16, C)[:, 0:12, :].astype(BF16)

    def scatter_rows(done, row):
        for lev in range(2):
            scatter = scatter_of(lev, False)
            for z in range(3):
                put(lev, z, row, dot(scatter, done[z * 2 * NC : (z + 1) * 2 * NC].astype(BF16)))

    pairs = [(z, side) for z in range(3) for side in range(2)]
    residual = [st[1 - first, z, 0:NB] + mix_b[1 - first, z * NB : (z + 1) * NB, :] for z in range(3)]
    residual += [st[side, z, NB:BC] + mix_c[side, z * NC : (z + 1) * NC, :] for z, side in pairs]
    done = feed_forward(jnp.concatenate(residual, axis=0), wu_v[...], wd_t[...])
    out_b[1 - first] = done[0 : 3 * NB]
    scatter_rows(done[3 * NB :], 9)
    for lev in range(2):
        scatter = scatter_of(lev, True)
        for z in range(3):
            part = pl.ds(z * NB, NB)
            tokens = jnp.concatenate([out_b[0, part], out_b[1, part]], axis=0).astype(BF16)
            put(lev, z, 3, dot(scatter, tokens))

    @pl.when(has_above)
    def _():
        down(0).wait_recv()
        down(1).wait_recv()

    @pl.when(jnp.logical_not(has_above))
    def _():
        r_ret[...] = jnp.zeros_like(r_ret)

    for side in range(2):
        unpack(ret_x.at[side], r_ret.at[side], HALVED)
    residual = [st[side, z, BC : BC + NC] + ret_x[side, z * NC : (z + 1) * NC, :].astype(F32) for z, side in pairs]
    scatter_rows(feed_forward(jnp.concatenate(residual, axis=0), wu_v[...], wd_t[...]), 0)

    for copy in (along_b, along_c):
        copy(0, left).wait_send()
        copy(1, right).wait_send()
    regions.wait_send()

    @pl.when(has_above)
    def _():
        for side, (far, col) in enumerate(sides):
            pl.when(far)(corner(side, m_lat, la - 1, col).wait_send)
        up.wait_send()

    @pl.when(has_below)
    def _():
        for side, (far, col) in enumerate(sides):
            pl.when(jnp.logical_not(far))(corner(side, r_lat, la, col).wait_send)
        down(0).wait_send()
        down(1).wait_send()


def shards(n_lat, n_lon, *args):
    args = (*args[:6], args[6].T)
    args = [pltpu.with_memory_space_constraint(a, pltpu.HBM) for a in args]
    def packed(form, *lead):
        return pltpu.VMEM((*lead, form[0] + form[1], 128), BF16)

    scratch = [
        pltpu.VMEM((6, 12, 12, C), BF16),
        pltpu.VMEM((2, HEADS, 144, 144), BF16),
        pltpu.VMEM((12, 12), jnp.int32),
        pltpu.VMEM((12, 12), jnp.int32),
        pltpu.VMEM((C, 3 * C), BF16),
        pltpu.VMEM((C, C), BF16),
        pltpu.VMEM((C, C), BF16),
        pltpu.VMEM((C, C), BF16),
        pltpu.VMEM((C, C), BF16),
        pltpu.VMEM((C, FF), BF16),
        pltpu.VMEM((C, FF), BF16),
        pltpu.VMEM((FF, C), BF16),
        pltpu.VMEM((6, 12, 16, C), F32),
        pltpu.VMEM((2, 3, BC + NC, C), F32),
        pltpu.VMEM((2, 224, C), F32),
        pltpu.VMEM((2, 128, C), F32),
        pltpu.VMEM((2, 128, C), F32),
        packed(FULL, 2),
        packed(HALVED, 2),
        packed(HALVED, 2),
        packed(HALVED, 2),
        packed(FULL, 2),
        packed(HALVED, 2),
        packed(HALVED, 2),
        packed(HALVED, 2),
        packed(HALVED, 2),
        pltpu.VMEM((2, 3, 224, C), F32),
        pltpu.VMEM((2, 3, 128, C), F32),
        pltpu.VMEM((224, C), BF16),
        pltpu.VMEM((128, C), BF16),
        pltpu.VMEM((2, 128, C), BF16),
        pltpu.VMEM((128, C), BF16),
        pltpu.VMEM((2, 224, C), F32),
        pltpu.VMEM((2, 128, C), F32),
        pltpu.VMEM((2, 128, C), F32),
        pltpu.VMEM((2, 128, C), F32),
        pltpu.VMEM((2, 128, C), F32),
        pltpu.VMEM((128, C), F32),
        pltpu.VMEM((128, C), F32),
        pltpu.VMEM((2, HEADS * NB, 2 * NB), F32),
        pltpu.VMEM((2, HEADS * 2 * NC, 4 * NC), F32),
        pltpu.VMEM((16, 128), F32),
        pltpu.VMEM((2, 3 * NB, C), F32),
        pltpu.VMEM((2, 3 * NC, C), F32),
        pltpu.VMEM((128, C), F32),
        pltpu.VMEM((2, 128, C), BF16),
        pltpu.VMEM((2, 3 * NB, C), F32),
        pltpu.SemaphoreType.DMA((7,)),
        pltpu.SemaphoreType.DMA((10,)),
        pltpu.SemaphoreType.DMA((10,)),
        pltpu.SemaphoreType.REGULAR,
    ]
    return pl.pallas_call(
        functools.partial(kernel, n_lat, n_lon),
        out_shape=pltpu.VMEM((6, 12, 12, C), BF16),
        in_specs=[pl.BlockSpec(memory_space=pltpu.HBM)] * 7,
        out_specs=pl.BlockSpec(memory_space=pltpu.VMEM),
        scratch_shapes=scratch,
        compiler_params=pltpu.CompilerParams(
            collective_id=0, has_side_effects=True, vmem_limit_bytes=40 * 1024 * 1024
        ),
    )(*args)


def solution(mesh):
    placed = (
        P(None, "lat", "lon", None),
        P("lat", None, None, None),
        P("lat", "lon"),
        P(),
        P(),
        P(),
        P(),
    )
    return jax.shard_map(
        functools.partial(shards, mesh.shape["lat"], mesh.shape["lon"]),
        mesh=mesh,
        in_specs=placed,
        out_specs=P(None, "lat", "lon", None),
        check_vma=False,
    )
```

```python
import functools

import jax
import jax.numpy as jnp
from jax import lax
from jax.experimental import pallas as pl
from jax.experimental.pallas import tpu as pltpu
from jax.sharding import PartitionSpec as P

HEADS = 6
C = 192
FF = 768
HALF = 6
NB = 72
NC = 40
BC = NB + NC
EPS = 1e-05
NEG = -1000000000.0
SCALE = 1.0 / 32**0.5
MESH = pl.DeviceIdType.MESH
F32 = jnp.float32
BF16 = jnp.bfloat16

FULL = (224, 112, 112)
HALVED = (128, 64, 64)


def dot(a, b):
    return jnp.dot(a, b, preferred_element_type=F32)


def dot_nt(a, b):
    return lax.dot_general(a, b, (((1,), (1,)), ((), ())), preferred_element_type=F32)


def dot_tt(a, b):
    return lax.dot_general(a, b, (((0,), (1,)), ((), ())), preferred_element_type=F32)


def dot_tn(a, b):
    return lax.dot_general(a, b, (((0,), (0,)), ((), ())), preferred_element_type=F32)


def layer_norm(values):
    average = jnp.mean(values, axis=-1, keepdims=True)
    centred = values - average
    variance = jnp.mean(centred * centred, axis=-1, keepdims=True)
    return centred * lax.rsqrt(variance + EPS)


def one_hot(hit):
    return jnp.where(hit, 1.0, 0.0).astype(BF16)


def iota(shape, axis):
    return lax.broadcasted_iota(jnp.int32, shape, axis)


def by36(t):
    return (t * 57) >> 11


def by18(t):
    return (t * 57) >> 10


def by6(t):
    return (t * 43) >> 8


def gather_of(side):
    t = iota((BC + NC, 1), 0)
    is_b = t < NB
    is_a = t >= BC
    u = jnp.where(is_a, t - BC, t - NB)
    lev = jnp.where(is_b, by36(t), by18(u))
    v = jnp.where(is_b, t - 36 * lev, u - 18 * lev)
    row = by6(v)
    col = v - 6 * row + HALF * side
    row = row + jnp.where(is_b, 3, jnp.where(is_a, 0, 9))
    source = lev * 192 + row * 16 + col
    source = jnp.where(is_b | (u < 36), source, -1)
    return one_hot(iota((BC + NC, 384), 1) == source)


def scatter_of(lev, full):
    rows, width = (6, NB) if full else (3, NC)
    d = iota((rows * 16, 1), 0)
    row, col = d >> 4, d & 15
    side = jnp.where(col >= HALF, 1, 0)
    source = side * width + lev * rows * HALF + row * HALF + col - HALF * side
    source = jnp.where(col < 12, source, -1)
    return one_hot(iota((rows * 16, 2 * width), 1) == source)


def key_place(t, band, side):
    if band == 0:
        halo = t >= NB
        u = jnp.where(halo, t - NB, t)
        lev = by36(u)
        v = u - 36 * lev
        row = by6(v)
        col = v - 6 * row
        valid = t >= 0
    else:
        halo = t >= 2 * NC
        w = jnp.where(halo, t - 2 * NC, t)
        below = w >= NC
        u = jnp.where(below, w - NC, w)
        lev = by18(u)
        v = u - 18 * lev
        row = by6(v)
        col = v - 6 * row
        row = row + jnp.where(below, 3, 0)
        valid = u < 36
    col = col + jnp.where(halo, HALF * side, HALF * (1 - side))
    return lev, row, col, valid


def pack(buf, x, form):
    tokens, rest, second = form
    buf[0:tokens, :] = x[:, 0:128].astype(BF16)
    low, high = x[0:rest, 128:192], x[second : second + rest, 128:192]
    buf[tokens : tokens + rest, :] = jnp.concatenate([low, high], axis=1).astype(BF16)


def unpack(dst, buf, form):
    tokens, rest, second = form
    dst[0:tokens, 0:128] = buf[0:tokens, :]
    tail = buf[tokens : tokens + rest, :]
    dst[0:rest, 128:192] = tail[:, 0:64]
    dst[second : second + rest, 128:192] = tail[:, 64:128]


def attend(windows):
    n = windows[0][0].shape[0]
    head = iota((1, C), 1) >> 5
    stacked = [jnp.concatenate([jnp.where(head == h, q, 0.0) for h in range(HEADS)], axis=0).astype(BF16) for q, *_ in windows]
    scores = [dot_nt(s, k) * SCALE + bias for s, (_, k, _, bias) in zip(stacked, windows)]
    tops = [jnp.max(s, axis=-1, keepdims=True) for s in scores]
    weights = [jnp.exp(s - t) for s, t in zip(scores, tops)]
    totals = [1.0 / jnp.sum(w, axis=-1, keepdims=True) for w in weights]
    outs = []
    for w, t, (_, _, v, _) in zip(weights, totals, windows):
        mixed = dot(w.astype(BF16), v) * t
        out = jnp.where(head == 0, mixed[0:n], 0.0)
        for h in range(1, HEADS):
            out = jnp.where(head == h, mixed[h * n : (h + 1) * n], out)
        outs.append(out)
    return outs


def feed_forward(residual, w_up, w_down):
    normed = layer_norm(residual).astype(BF16)
    hidden = jax.nn.gelu(dot(normed, w_up)).astype(BF16)
    return residual + dot(hidden, w_down)


def kernel(
    n_lat,
    n_lon,
    state,
    attn_bias,
    region_ids,
    w_qkv,
    w_out,
    w_up,
    w_down,
    out,
    x_in,
    bias_in,
    region,
    region_left,
    wqkv_v,
    wq,
    wk,
    wv,
    wo_v,
    wu_v,
    wd_v,
    wd_t,
    xp,
    st,
    normed_b,
    normed_c,
    normed_a,
    m_b,
    m_c,
    m_lat,
    m_ret,
    r_b,
    r_c,
    r_lat,
    r_diag,
    r_ret,
    own_b,
    own_c,
    halo_bx,
    halo_cx,
    lat_x,
    diag_x,
    halo_b,
    halo_c,
    lat_q,
    lat_k,
    lat_v,
    diag_k,
    diag_v,
    bias_b,
    bias_c,
    labels,
    mix_b,
    mix_c,
    mix_ret,
    ret_x,
    out_b,
    load_sem,
    send_sem,
    recv_sem,
    here_sem,
):
    la = lax.axis_index("lat")
    lo = lax.axis_index("lon")
    right = lax.rem(lo + 1, n_lon)
    left = lax.rem(lo + n_lon - 1, n_lon)
    has_above = la > 0
    has_below = la < n_lat - 1
    half = n_lon // 2
    far_left = lax.rem(lo, half) == 0
    far_right = lax.rem(lo + 1, half) == 0
    end = far_left | far_right
    end_on_left = lax.rem(lo + half - 1, half) == 0
    end_on_right = lax.rem(lo + 2, half) == 0
    mate = end_on_left | end_on_right
    near = jnp.where(far_left, right, jnp.where(far_right, left, lo))
    sides = ((far_left, left), (far_right, right))

    barrier = pltpu.get_barrier_semaphore()

    def greet(row, col):
        pl.semaphore_signal(barrier, inc=1, device_id=(row, col), device_id_type=MESH)

    pl.when(jnp.logical_not(end_on_left))(functools.partial(greet, la, left))
    pl.when(jnp.logical_not(end_on_right))(functools.partial(greet, la, right))
    for there, row in ((has_above, la - 1), (has_below, la + 1)):
        pl.when(there)(functools.partial(greet, row, near))
        for far, col in sides:
            pl.when(there & far)(functools.partial(greet, row, col))

    loads = [
        pltpu.make_async_copy(src, dst, load_sem.at[i])
        for i, (src, dst) in enumerate(
            [
                (state, x_in),
                (w_qkv, wqkv_v),
                (attn_bias, bias_in),
                (region_ids, region),
                (w_out, wo_v),
                (w_up, wu_v),
                (w_down, wd_v),
            ]
        )
    ]
    for load in loads:
        load.start()

    xp[...] = jnp.zeros_like(xp)
    for ref in (normed_a, normed_b, normed_c):
        ref[...] = jnp.zeros_like(ref)
    mix_ret[...] = jnp.zeros_like(mix_ret)
    gathers = [gather_of(0), gather_of(1)]
    loads[0].wait()
    for lev in range(6):
        xp[lev, :, 0:12, :] = x_in[(lev + 1) % 6].astype(F32)
    for z in range(3):
        tokens = xp[2 * z : 2 * z + 2].reshape(384, C).astype(BF16)
        for side in range(2):
            x = dot(gathers[side], tokens)
            st[side, z] = x
            x = layer_norm(x)
            normed_b[side, z * NB : (z + 1) * NB, :] = x[0:NB]
            normed_c[side, z * NC : (z + 1) * NC, :] = x[NB:BC]
            normed_a[side, z * NC : (z + 1) * NC, :] = x[BC : BC + NC]
    for side in range(2):
        pack(m_b.at[side], normed_b[side], FULL)
        pack(m_c.at[side], normed_c[side], HALVED)
        pack(m_lat.at[side], normed_a[side], HALVED)

    def remote(src, dst, i, device):
        return pltpu.make_async_remote_copy(
            src_ref=src,
            dst_ref=dst,
            send_sem=send_sem.at[i],
            recv_sem=recv_sem.at[i],
            device_id=device,
            device_id_type=MESH,
        )

    def along_b(side, col):
        return remote(m_b.at[side], r_b.at[1 - side], 1 - side, (la, col))

    def along_c(side, col):
        return remote(m_c.at[side], r_c.at[1 - side], 9 - side, (la, col))

    def corner(side, source, row, col):
        return remote(source.at[side], r_diag.at[1 - side], 3 - side, (row, col))

    regions = remote(region_ids, region_left, 4, (la, right))
    up = remote(m_lat, r_lat, 5, (la - 1, lo))

    rows = jnp.where(has_above, 1, 0) + jnp.where(has_below, 1, 0)

    def send_near():
        @pl.when(jnp.logical_not(end))
        def _():
            pl.semaphore_wait(barrier, 2 + rows * jnp.where(mate, 2, 1))

        @pl.when(mate)
        def _():
            col = jnp.where(end_on_left, left, right)
            pl.semaphore_signal(here_sem, inc=1, device_id=(la, col), device_id_type=MESH)

        @pl.when(end)
        def _():
            pl.semaphore_wait(here_sem, 1)

        pl.when(has_above)(up.start)
        pl.when(jnp.logical_not(far_right))(regions.start)
        for side, (far, col) in enumerate(sides):
            pl.when(jnp.logical_not(far))(along_b(side, col).start)
            pl.when(jnp.logical_not(far))(along_c(side, col).start)

    def send_far():
        pl.semaphore_wait(barrier, 1 + rows)
        pl.when(far_right)(regions.start)
        for side, (far, col) in enumerate(sides):
            pl.when(far & has_above)(corner(side, m_lat, la - 1, col).start)
            pl.when(far)(along_c(side, col).start)
            pl.when(far)(along_b(side, col).start)

    def prepare():
        loads[1].wait()
        wq[...] = wqkv_v[:, 0:192]
        wk[...] = wqkv_v[:, 192:384]
        wv[...] = wqkv_v[:, 384:576]
        for side in range(2):
            for own, normed in ((own_b, normed_b), (own_c, normed_c)):
                x = normed[side].astype(BF16)
                for i, w in enumerate((wq, wk, wv)):
                    own[side, i] = dot(x, w[...])
        loads[2].wait()
        for band, (store, n, m) in enumerate(((bias_b, NB, 2 * NB), (bias_c, 2 * NC, 4 * NC))):
            for side in range(2):
                lev, row, col, valid = key_place(iota((n, 1), 0), band, side)
                at = jnp.where(valid, lev * 72 + row * 12 + col, -1)
                select = one_hot(iota((n, 144), 1) == at)
                rows = [dot(select, bias_in[band, h]) for h in range(HEADS)]
                rows = jnp.concatenate(rows, axis=0).astype(BF16)
                lev, row, col, valid = key_place(iota((1, m), 1), band, side)
                at = jnp.where(valid, lev * 72 + row * 12 + col, -1)
                store[side] = dot(rows, one_hot(iota((144, m), 0) == at))
        loads[3].wait()
        apply_mask(1, region)
        loads[6].wait()
        wd_t[...] = wd_v[...].T

    def apply_mask(side, source):
        labels[...] = jnp.zeros_like(labels)
        labels[0:12, 0:12] = source[...].astype(F32)
        table = labels[...].astype(BF16)
        for band, (store, n, m) in enumerate(((bias_b, NB, 2 * NB), (bias_c, 2 * NC, 4 * NC))):
            _, row, col, _ = key_place(iota((m, 1), 0), band, side)
            in_row = one_hot(iota((m, 16), 1) == row + 6 * band)
            queries = dot(in_row[0:n], table)
            queries = jnp.where(iota((n, 128), 1) == col[0:n], queries, 0.0)
            queries = jnp.sum(queries, axis=1, keepdims=True)
            _, row, col, valid = key_place(iota((1, m), 1), band, side)
            keys = dot_tt(table, in_row)
            keys = jnp.where(iota((128, m), 0) == col, keys, 0.0)
            keys = jnp.sum(keys, axis=0, keepdims=True)
            valid = valid & (la * 12 + 6 * band + row < n_lat * 12 - 3)
            keys = jnp.where(valid, keys, -1.0)
            allowed = queries == keys
            for h in range(HEADS):
                part = store[side, h * n : (h + 1) * n, :]
                store[side, h * n : (h + 1) * n, :] = jnp.where(allowed, part, NEG)

    def start(i, carry):
        far_first = lo >= half
        pl.when(i == jnp.where(far_first, 1, 0))(send_near)
        pl.when(end & (i == jnp.where(far_first, 0, 2)))(send_far)
        pl.when(i == jnp.where(far_first, 2, 1))(prepare)
        return carry

    lax.fori_loop(0, 3, start, 0)

    loads[4].wait()
    loads[5].wait()

    def down(side):
        return remote(m_ret.at[side], r_ret.at[side], 6 + side, (la + 1, lo))

    def mask():
        regions.wait_recv()
        apply_mask(0, region_left)

    def halo(copy, x_ref, buf, keys_values, form):
        copy.wait_recv()
        unpack(x_ref, buf, form)
        x = x_ref[...]
        keys_values[0] = dot(x, wk[...])
        keys_values[1] = dot(x, wv[...])

    def rows_below():
        @pl.when(has_below)
        def _():
            up.wait_recv()
            for side, (far, col) in enumerate(sides):
                pl.when(jnp.logical_not(far))(corner(side, r_lat, la, col).start)

        @pl.when(jnp.logical_not(has_below))
        def _():
            r_lat[...] = jnp.zeros_like(r_lat)
            r_diag[...] = jnp.zeros_like(r_diag)

        for side in range(2):
            unpack(lat_x.at[side], r_lat.at[side], HALVED)
            x = lat_x[side]
            lat_q[side] = dot(x, wq[...])
            lat_k[side] = dot(x, wk[...])
            lat_v[side] = dot(x, wv[...])

    def windows_c(side):
        @pl.when(has_below)
        def _():
            corner(1 - side, r_lat, la, left).wait_recv()

        halo(along_c(1 - side, left), halo_cx, r_c.at[side], halo_c, HALVED)
        unpack(diag_x, r_diag.at[side], HALVED)
        x = diag_x[...]
        diag_k[...] = dot(x, wk[...])
        diag_v[...] = dot(x, wv[...])
        windows = []
        for z in range(3):
            a = pl.ds(z * NC, NC)
            q = jnp.concatenate([own_c[side, 0, a], lat_q[side, a]], axis=0)
            k = jnp.concatenate([own_c[side, 1, a], lat_k[side, a], halo_c[0, a], diag_k[a]], axis=0)
            v = jnp.concatenate([own_c[side, 2, a], lat_v[side, a], halo_c[1, a], diag_v[a]], axis=0)
            windows.append((q, k.astype(BF16), v.astype(BF16), bias_c[side]))
        context = jnp.concatenate(attend(windows), axis=0)
        mixed = dot(context.astype(BF16), wo_v[...]).astype(BF16).astype(F32)
        for z in range(3):
            at = z * 2 * NC
            mix_c[side, z * NC : (z + 1) * NC, :] = mixed[at : at + NC]
            mix_ret[z * NC : (z + 1) * NC, :] = mixed[at + NC : at + 2 * NC]
        pack(m_ret.at[side], mix_ret[...], HALVED)

        @pl.when(has_below)
        def _():
            down(side).start()

    def windows_b(side):
        halo(along_b(1 - side, left), halo_bx, r_b.at[side], halo_b, FULL)
        windows = []
        for z in range(3):
            b = pl.ds(z * NB, NB)
            k = jnp.concatenate([own_b[side, 1, b], halo_b[0, b]], axis=0)
            v = jnp.concatenate([own_b[side, 2, b], halo_b[1, b]], axis=0)
            windows.append((own_b[side, 0, b], k.astype(BF16), v.astype(BF16), bias_b[side]))
        context = jnp.concatenate(attend(windows), axis=0)
        mixed = dot(context.astype(BF16), wo_v[...]).astype(BF16).astype(F32)
        for z in range(3):
            mix_b[side, z * NB : (z + 1) * NB, :] = mixed[z * NB : (z + 1) * NB]

    def feed_b(side):
        residual = jnp.concatenate([st[side, z, 0:NB] for z in range(3)], axis=0) + mix_b[side]
        out_b[side] = feed_forward(residual, wu_v[...], wd_t[...])

    late = lax.rem(la, 4) == 3
    inner = late & jnp.logical_not(end)
    first_right = far_left | end_on_left
    first = jnp.where(first_right, 1, 0)
    at_c = (jnp.where(inner, 4, jnp.where(late, 2, 1)), jnp.where(inner, 5, 3))
    at_b = (0, jnp.where(inner, 1, 4))
    at_feed = jnp.where(late & end, 1, jnp.where(inner, 3, 2))

    def task(step, carry):
        second = (step == at_c[1]) | (step == at_b[1])
        side = jnp.where(second, 1 - first, first)
        pl.when(step == at_feed)(functools.partial(feed_b, side))
        pl.when(step == jnp.where(first_right, jnp.where(inner, 1, 2), 0))(mask)
        pl.when(step == jnp.where(late, at_c[0], 0))(rows_below)
        pl.when((step == at_c[0]) | (step == at_c[1]))(functools.partial(windows_c, side))
        pl.when((step == at_b[0]) | (step == at_b[1]))(functools.partial(windows_b, side))
        return carry

    lax.fori_loop(0, 6, task, 0)

    def put(lev, z, row, grid):
        rows = grid.shape[0] // 16
        out[(2 * z + lev + 1) % 6, row : row + rows] = grid.reshape(rows, 16, C)[:, 0:12, :].astype(BF16)

    def scatter_rows(done, row):
        for lev in range(2):
            scatter = scatter_of(lev, False)
            for z in range(3):
                put(lev, z, row, dot(scatter, done[z * 2 * NC : (z + 1) * 2 * NC].astype(BF16)))

    pairs = [(z, side) for z in range(3) for side in range(2)]
    residual = [st[1 - first, z, 0:NB] + mix_b[1 - first, z * NB : (z + 1) * NB, :] for z in range(3)]
    residual += [st[side, z, NB:BC] + mix_c[side, z * NC : (z + 1) * NC, :] for z, side in pairs]
    done = feed_forward(jnp.concatenate(residual, axis=0), wu_v[...], wd_t[...])
    out_b[1 - first] = done[0 : 3 * NB]
    scatter_rows(done[3 * NB :], 9)
    for lev in range(2):
        scatter = scatter_of(lev, True)
        for z in range(3):
            part = pl.ds(z * NB, NB)
            tokens = jnp.concatenate([out_b[0, part], out_b[1, part]], axis=0).astype(BF16)
            put(lev, z, 3, dot(scatter, tokens))

    @pl.when(has_above)
    def _():
        down(0).wait_recv()
        down(1).wait_recv()

    @pl.when(jnp.logical_not(has_above))
    def _():
        r_ret[...] = jnp.zeros_like(r_ret)

    for side in range(2):
        unpack(ret_x.at[side], r_ret.at[side], HALVED)
    residual = [st[side, z, BC : BC + NC] + ret_x[side, z * NC : (z + 1) * NC, :].astype(F32) for z, side in pairs]
    scatter_rows(feed_forward(jnp.concatenate(residual, axis=0), wu_v[...], wd_t[...]), 0)

    for copy in (along_b, along_c):
        copy(0, left).wait_send()
        copy(1, right).wait_send()
    regions.wait_send()

    @pl.when(has_above)
    def _():
        for side, (far, col) in enumerate(sides):
            pl.when(far)(corner(side, m_lat, la - 1, col).wait_send)
        up.wait_send()

    @pl.when(has_below)
    def _():
        for side, (far, col) in enumerate(sides):
            pl.when(jnp.logical_not(far))(corner(side, r_lat, la, col).wait_send)
        down(0).wait_send()
        down(1).wait_send()


def shards(n_lat, n_lon, *args):
    args = (*args[:6], args[6].T)
    args = [pltpu.with_memory_space_constraint(a, pltpu.HBM) for a in args]
    def packed(form, *lead):
        return pltpu.VMEM((*lead, form[0] + form[1], 128), BF16)

    scratch = [
        pltpu.VMEM((6, 12, 12, C), BF16),
        pltpu.VMEM((2, HEADS, 144, 144), BF16),
        pltpu.VMEM((12, 12), jnp.int32),
        pltpu.VMEM((12, 12), jnp.int32),
        pltpu.VMEM((C, 3 * C), BF16),
        pltpu.VMEM((C, C), BF16),
        pltpu.VMEM((C, C), BF16),
        pltpu.VMEM((C, C), BF16),
        pltpu.VMEM((C, C), BF16),
        pltpu.VMEM((C, FF), BF16),
        pltpu.VMEM((C, FF), BF16),
        pltpu.VMEM((FF, C), BF16),
        pltpu.VMEM((6, 12, 16, C), F32),
        pltpu.VMEM((2, 3, BC + NC, C), F32),
        pltpu.VMEM((2, 224, C), F32),
        pltpu.VMEM((2, 128, C), F32),
        pltpu.VMEM((2, 128, C), F32),
        packed(FULL, 2),
        packed(HALVED, 2),
        packed(HALVED, 2),
        packed(HALVED, 2),
        packed(FULL, 2),
        packed(HALVED, 2),
        packed(HALVED, 2),
        packed(HALVED, 2),
        packed(HALVED, 2),
        pltpu.VMEM((2, 3, 224, C), F32),
        pltpu.VMEM((2, 3, 128, C), F32),
        pltpu.VMEM((224, C), BF16),
        pltpu.VMEM((128, C), BF16),
        pltpu.VMEM((2, 128, C), BF16),
        pltpu.VMEM((128, C), BF16),
        pltpu.VMEM((2, 224, C), F32),
        pltpu.VMEM((2, 128, C), F32),
        pltpu.VMEM((2, 128, C), F32),
        pltpu.VMEM((2, 128, C), F32),
        pltpu.VMEM((2, 128, C), F32),
        pltpu.VMEM((128, C), F32),
        pltpu.VMEM((128, C), F32),
        pltpu.VMEM((2, HEADS * NB, 2 * NB), F32),
        pltpu.VMEM((2, HEADS * 2 * NC, 4 * NC), F32),
        pltpu.VMEM((16, 128), F32),
        pltpu.VMEM((2, 3 * NB, C), F32),
        pltpu.VMEM((2, 3 * NC, C), F32),
        pltpu.VMEM((128, C), F32),
        pltpu.VMEM((2, 128, C), BF16),
        pltpu.VMEM((2, 3 * NB, C), F32),
        pltpu.SemaphoreType.DMA((7,)),
        pltpu.SemaphoreType.DMA((10,)),
        pltpu.SemaphoreType.DMA((10,)),
        pltpu.SemaphoreType.REGULAR,
    ]
    return pl.pallas_call(
        functools.partial(kernel, n_lat, n_lon),
        out_shape=pltpu.VMEM((6, 12, 12, C), BF16),
        in_specs=[pl.BlockSpec(memory_space=pltpu.HBM)] * 7,
        out_specs=pl.BlockSpec(memory_space=pltpu.VMEM),
        scratch_shapes=scratch,
        compiler_params=pltpu.CompilerParams(
            collective_id=0, has_side_effects=True, vmem_limit_bytes=40 * 1024 * 1024
        ),
    )(*args)


def solution(mesh):
    placed = (
        P(None, "lat", "lon", None),
        P("lat", None, None, None),
        P("lat", "lon"),
        P(),
        P(),
        P(),
        P(),
    )
    return jax.shard_map(
        functools.partial(shards, mesh.shape["lat"], mesh.shape["lon"]),
        mesh=mesh,
        in_specs=placed,
        out_specs=P(None, "lat", "lon", None),
        check_vma=False,
    )
```

```python
import functools

import jax
import jax.numpy as jnp
from jax import lax
from jax.experimental import pallas as pl
from jax.experimental.pallas import tpu as pltpu
from jax.sharding import PartitionSpec as P

HEADS = 6
C = 192
FF = 768
HALF = 6
NB = 72
NC = 40
BC = NB + NC
EPS = 1e-05
NEG = -1000000000.0
SCALE = 1.0 / 32**0.5
MESH = pl.DeviceIdType.MESH
F32 = jnp.float32
BF16 = jnp.bfloat16

FULL = (224, 112, 112)
HALVED = (128, 64, 64)


def dot(a, b):
    return jnp.dot(a, b, preferred_element_type=F32)


def dot_nt(a, b):
    return lax.dot_general(a, b, (((1,), (1,)), ((), ())), preferred_element_type=F32)


def dot_tt(a, b):
    return lax.dot_general(a, b, (((0,), (1,)), ((), ())), preferred_element_type=F32)


def dot_tn(a, b):
    return lax.dot_general(a, b, (((0,), (0,)), ((), ())), preferred_element_type=F32)


def layer_norm(values):
    average = jnp.mean(values, axis=-1, keepdims=True)
    centred = values - average
    variance = jnp.mean(centred * centred, axis=-1, keepdims=True)
    return centred * lax.rsqrt(variance + EPS)


def one_hot(hit):
    return jnp.where(hit, 1.0, 0.0).astype(BF16)


def iota(shape, axis):
    return lax.broadcasted_iota(jnp.int32, shape, axis)


def by36(t):
    return (t * 57) >> 11


def by18(t):
    return (t * 57) >> 10


def by6(t):
    return (t * 43) >> 8


def gather_of(side):
    t = iota((BC + NC, 1), 0)
    is_b = t < NB
    is_a = t >= BC
    u = jnp.where(is_a, t - BC, t - NB)
    lev = jnp.where(is_b, by36(t), by18(u))
    v = jnp.where(is_b, t - 36 * lev, u - 18 * lev)
    row = by6(v)
    col = v - 6 * row + HALF * side
    row = row + jnp.where(is_b, 3, jnp.where(is_a, 0, 9))
    source = lev * 192 + row * 16 + col
    source = jnp.where(is_b | (u < 36), source, -1)
    return one_hot(iota((BC + NC, 384), 1) == source)


def scatter_of(lev, full):
    rows, width = (6, NB) if full else (3, NC)
    d = iota((rows * 16, 1), 0)
    row, col = d >> 4, d & 15
    side = jnp.where(col >= HALF, 1, 0)
    source = side * width + lev * rows * HALF + row * HALF + col - HALF * side
    source = jnp.where(col < 12, source, -1)
    return one_hot(iota((rows * 16, 2 * width), 1) == source)


def key_place(t, band, side):
    if band == 0:
        halo = t >= NB
        u = jnp.where(halo, t - NB, t)
        lev = by36(u)
        v = u - 36 * lev
        row = by6(v)
        col = v - 6 * row
        valid = t >= 0
    else:
        halo = t >= 2 * NC
        w = jnp.where(halo, t - 2 * NC, t)
        below = w >= NC
        u = jnp.where(below, w - NC, w)
        lev = by18(u)
        v = u - 18 * lev
        row = by6(v)
        col = v - 6 * row
        row = row + jnp.where(below, 3, 0)
        valid = u < 36
    col = col + jnp.where(halo, HALF * side, HALF * (1 - side))
    return lev, row, col, valid


def pack(buf, x, form):
    tokens, rest, second = form
    buf[0:tokens, :] = x[:, 0:128].astype(BF16)
    low, high = x[0:rest, 128:192], x[second : second + rest, 128:192]
    buf[tokens : tokens + rest, :] = jnp.concatenate([low, high], axis=1).astype(BF16)


def unpack(dst, buf, form):
    tokens, rest, second = form
    dst[0:tokens, 0:128] = buf[0:tokens, :]
    tail = buf[tokens : tokens + rest, :]
    dst[0:rest, 128:192] = tail[:, 0:64]
    dst[second : second + rest, 128:192] = tail[:, 64:128]


def attend(windows):
    n = windows[0][0].shape[0]
    head = iota((1, C), 1) >> 5
    stacked = [jnp.concatenate([jnp.where(head == h, q, 0.0) for h in range(HEADS)], axis=0).astype(BF16) for q, *_ in windows]
    scores = [dot_nt(s, k) * SCALE + bias for s, (_, k, _, bias) in zip(stacked, windows)]
    tops = [jnp.max(s, axis=-1, keepdims=True) for s in scores]
    weights = [jnp.exp(s - t) for s, t in zip(scores, tops)]
    totals = [1.0 / jnp.sum(w, axis=-1, keepdims=True) for w in weights]
    outs = []
    for w, t, (_, _, v, _) in zip(weights, totals, windows):
        mixed = dot(w.astype(BF16), v) * t
        out = jnp.where(head == 0, mixed[0:n], 0.0)
        for h in range(1, HEADS):
            out = jnp.where(head == h, mixed[h * n : (h + 1) * n], out)
        outs.append(out)
    return outs


def feed_forward(residual, w_up, w_down):
    normed = layer_norm(residual).astype(BF16)
    hidden = jax.nn.gelu(dot(normed, w_up)).astype(BF16)
    return residual + dot(hidden, w_down)


def kernel(
    n_lat,
    n_lon,
    state,
    attn_bias,
    region_ids,
    w_qkv,
    w_out,
    w_up,
    w_down,
    out,
    x_in,
    bias_in,
    region,
    region_left,
    wqkv_v,
    wq,
    wk,
    wv,
    wo_v,
    wu_v,
    wd_v,
    wd_t,
    xp,
    st,
    normed_b,
    normed_c,
    normed_a,
    m_b,
    m_c,
    m_lat,
    m_ret,
    r_b,
    r_c,
    r_lat,
    r_diag,
    r_ret,
    own_b,
    own_c,
    halo_bx,
    halo_cx,
    lat_x,
    diag_x,
    halo_b,
    halo_c,
    lat_q,
    lat_k,
    lat_v,
    diag_k,
    diag_v,
    bias_b,
    bias_c,
    labels,
    mix_b,
    mix_c,
    mix_ret,
    ret_x,
    out_b,
    load_sem,
    send_sem,
    recv_sem,
    here_sem,
):
    la = lax.axis_index("lat")
    lo = lax.axis_index("lon")
    right = lax.rem(lo + 1, n_lon)
    left = lax.rem(lo + n_lon - 1, n_lon)
    has_above = la > 0
    has_below = la < n_lat - 1
    half = n_lon // 2
    far_left = lax.rem(lo, half) == 0
    far_right = lax.rem(lo + 1, half) == 0
    end = far_left | far_right
    end_on_left = lax.rem(lo + half - 1, half) == 0
    end_on_right = lax.rem(lo + 2, half) == 0
    mate = end_on_left | end_on_right
    near = jnp.where(far_left, right, jnp.where(far_right, left, lo))
    sides = ((far_left, left), (far_right, right))

    barrier = pltpu.get_barrier_semaphore()

    def greet(row, col):
        pl.semaphore_signal(barrier, inc=1, device_id=(row, col), device_id_type=MESH)

    pl.when(jnp.logical_not(end_on_left))(functools.partial(greet, la, left))
    pl.when(jnp.logical_not(end_on_right))(functools.partial(greet, la, right))
    for there, row in ((has_above, la - 1), (has_below, la + 1)):
        pl.when(there)(functools.partial(greet, row, near))
        for far, col in sides:
            pl.when(there & far)(functools.partial(greet, row, col))

    loads = [
        pltpu.make_async_copy(src, dst, load_sem.at[i])
        for i, (src, dst) in enumerate(
            [
                (state, x_in),
                (w_qkv, wqkv_v),
                (attn_bias, bias_in),
                (region_ids, region),
                (w_out, wo_v),
                (w_up, wu_v),
                (w_down, wd_v),
            ]
        )
    ]
    for load in loads:
        load.start()

    xp[...] = jnp.zeros_like(xp)
    for ref in (normed_a, normed_b, normed_c):
        ref[...] = jnp.zeros_like(ref)
    mix_ret[...] = jnp.zeros_like(mix_ret)
    gathers = [gather_of(0), gather_of(1)]
    loads[0].wait()
    for lev in range(6):
        xp[lev, :, 0:12, :] = x_in[(lev + 1) % 6].astype(F32)
    for z in range(3):
        tokens = xp[2 * z : 2 * z + 2].reshape(384, C).astype(BF16)
        for side in range(2):
            x = dot(gathers[side], tokens)
            st[side, z] = x
            x = layer_norm(x)
            normed_b[side, z * NB : (z + 1) * NB, :] = x[0:NB]
            normed_c[side, z * NC : (z + 1) * NC, :] = x[NB:BC]
            normed_a[side, z * NC : (z + 1) * NC, :] = x[BC : BC + NC]
    for side in range(2):
        pack(m_b.at[side], normed_b[side], FULL)
        pack(m_c.at[side], normed_c[side], HALVED)
        pack(m_lat.at[side], normed_a[side], HALVED)

    def remote(src, dst, i, device):
        return pltpu.make_async_remote_copy(
            src_ref=src,
            dst_ref=dst,
            send_sem=send_sem.at[i],
            recv_sem=recv_sem.at[i],
            device_id=device,
            device_id_type=MESH,
        )

    def along_b(side, col):
        return remote(m_b.at[side], r_b.at[1 - side], 1 - side, (la, col))

    def along_c(side, col):
        return remote(m_c.at[side], r_c.at[1 - side], 9 - side, (la, col))

    def corner(side, source, row, col):
        return remote(source.at[side], r_diag.at[1 - side], 3 - side, (row, col))

    regions = remote(region_ids, region_left, 4, (la, right))
    up = remote(m_lat, r_lat, 5, (la - 1, lo))

    rows = jnp.where(has_above, 1, 0) + jnp.where(has_below, 1, 0)

    def send_near():
        @pl.when(jnp.logical_not(end))
        def _():
            pl.semaphore_wait(barrier, 2 + rows * jnp.where(mate, 2, 1))

        @pl.when(mate)
        def _():
            col = jnp.where(end_on_left, left, right)
            pl.semaphore_signal(here_sem, inc=1, device_id=(la, col), device_id_type=MESH)

        @pl.when(end)
        def _():
            pl.semaphore_wait(here_sem, 1)

        pl.when(has_above)(up.start)
        pl.when(jnp.logical_not(far_right))(regions.start)
        for side, (far, col) in enumerate(sides):
            pl.when(jnp.logical_not(far))(along_b(side, col).start)
            pl.when(jnp.logical_not(far))(along_c(side, col).start)

    def send_far():
        pl.semaphore_wait(barrier, 1 + rows)
        pl.when(far_right)(regions.start)
        for side, (far, col) in enumerate(sides):
            pl.when(far & has_above)(corner(side, m_lat, la - 1, col).start)
            pl.when(far)(along_c(side, col).start)
            pl.when(far)(along_b(side, col).start)

    def prepare():
        loads[1].wait()
        wq[...] = wqkv_v[:, 0:192]
        wk[...] = wqkv_v[:, 192:384]
        wv[...] = wqkv_v[:, 384:576]
        for side in range(2):
            for own, normed in ((own_b, normed_b), (own_c, normed_c)):
                x = normed[side].astype(BF16)
                for i, w in enumerate((wq, wk, wv)):
                    own[side, i] = dot(x, w[...])
        loads[2].wait()
        for band, (store, n, m) in enumerate(((bias_b, NB, 2 * NB), (bias_c, 2 * NC, 4 * NC))):
            for side in range(2):
                lev, row, col, valid = key_place(iota((n, 1), 0), band, side)
                at = jnp.where(valid, lev * 72 + row * 12 + col, -1)
                select = one_hot(iota((n, 144), 1) == at)
                rows = [dot(select, bias_in[band, h]) for h in range(HEADS)]
                rows = jnp.concatenate(rows, axis=0).astype(BF16)
                lev, row, col, valid = key_place(iota((1, m), 1), band, side)
                at = jnp.where(valid, lev * 72 + row * 12 + col, -1)
                store[side] = dot(rows, one_hot(iota((144, m), 0) == at))
        loads[3].wait()
        apply_mask(1, region)
        loads[6].wait()
        wd_t[...] = wd_v[...].T

    def apply_mask(side, source):
        labels[...] = jnp.zeros_like(labels)
        labels[0:12, 0:12] = source[...].astype(F32)
        table = labels[...].astype(BF16)
        for band, (store, n, m) in enumerate(((bias_b, NB, 2 * NB), (bias_c, 2 * NC, 4 * NC))):
            _, row, col, _ = key_place(iota((m, 1), 0), band, side)
            in_row = one_hot(iota((m, 16), 1) == row + 6 * band)
            queries = dot(in_row[0:n], table)
            queries = jnp.where(iota((n, 128), 1) == col[0:n], queries, 0.0)
            queries = jnp.sum(queries, axis=1, keepdims=True)
            _, row, col, valid = key_place(iota((1, m), 1), band, side)
            keys = dot_tt(table, in_row)
            keys = jnp.where(iota((128, m), 0) == col, keys, 0.0)
            keys = jnp.sum(keys, axis=0, keepdims=True)
            valid = valid & (la * 12 + 6 * band + row < n_lat * 12 - 3)
            keys = jnp.where(valid, keys, -1.0)
            allowed = queries == keys
            for h in range(HEADS):
                part = store[side, h * n : (h + 1) * n, :]
                store[side, h * n : (h + 1) * n, :] = jnp.where(allowed, part, NEG)

    def start(i, carry):
        far_first = lo >= half
        pl.when(i == jnp.where(far_first, 1, 0))(send_near)
        pl.when(end & (i == jnp.where(far_first, 0, 2)))(send_far)
        pl.when(i == jnp.where(far_first, 2, 1))(prepare)
        return carry

    lax.fori_loop(0, 3, start, 0)

    loads[4].wait()
    loads[5].wait()

    def down(side):
        return remote(m_ret.at[side], r_ret.at[side], 6 + side, (la + 1, lo))

    def mask():
        regions.wait_recv()
        apply_mask(0, region_left)

    def halo(copy, x_ref, buf, keys_values, form):
        copy.wait_recv()
        unpack(x_ref, buf, form)
        x = x_ref[...]
        keys_values[0] = dot(x, wk[...])
        keys_values[1] = dot(x, wv[...])

    def rows_below():
        @pl.when(has_below)
        def _():
            up.wait_recv()
            for side, (far, col) in enumerate(sides):
                pl.when(jnp.logical_not(far))(corner(side, r_lat, la, col).start)

        @pl.when(jnp.logical_not(has_below))
        def _():
            r_lat[...] = jnp.zeros_like(r_lat)
            r_diag[...] = jnp.zeros_like(r_diag)

        for side in range(2):
            unpack(lat_x.at[side], r_lat.at[side], HALVED)
            x = lat_x[side]
            lat_q[side] = dot(x, wq[...])
            lat_k[side] = dot(x, wk[...])
            lat_v[side] = dot(x, wv[...])

    def windows_c(side):
        @pl.when(has_below)
        def _():
            corner(1 - side, r_lat, la, left).wait_recv()

        halo(along_c(1 - side, left), halo_cx, r_c.at[side], halo_c, HALVED)
        unpack(diag_x, r_diag.at[side], HALVED)
        x = diag_x[...]
        diag_k[...] = dot(x, wk[...])
        diag_v[...] = dot(x, wv[...])
        windows = []
        for z in range(3):
            a = pl.ds(z * NC, NC)
            q = jnp.concatenate([own_c[side, 0, a], lat_q[side, a]], axis=0)
            k = jnp.concatenate([own_c[side, 1, a], lat_k[side, a], halo_c[0, a], diag_k[a]], axis=0)
            v = jnp.concatenate([own_c[side, 2, a], lat_v[side, a], halo_c[1, a], diag_v[a]], axis=0)
            windows.append((q, k.astype(BF16), v.astype(BF16), bias_c[side]))
        context = jnp.concatenate(attend(windows), axis=0)
        mixed = dot(context.astype(BF16), wo_v[...]).astype(BF16).astype(F32)
        for z in range(3):
            at = z * 2 * NC
            mix_c[side, z * NC : (z + 1) * NC, :] = mixed[at : at + NC]
            mix_ret[z * NC : (z + 1) * NC, :] = mixed[at + NC : at + 2 * NC]
        pack(m_ret.at[side], mix_ret[...], HALVED)

        @pl.when(has_below)
        def _():
            down(side).start()

    def windows_b(side):
        halo(along_b(1 - side, left), halo_bx, r_b.at[side], halo_b, FULL)
        windows = []
        for z in range(3):
            b = pl.ds(z * NB, NB)
            k = jnp.concatenate([own_b[side, 1, b], halo_b[0, b]], axis=0)
            v = jnp.concatenate([own_b[side, 2, b], halo_b[1, b]], axis=0)
            windows.append((own_b[side, 0, b], k.astype(BF16), v.astype(BF16), bias_b[side]))
        context = jnp.concatenate(attend(windows), axis=0)
        mixed = dot(context.astype(BF16), wo_v[...]).astype(BF16).astype(F32)
        for z in range(3):
            mix_b[side, z * NB : (z + 1) * NB, :] = mixed[z * NB : (z + 1) * NB]

    def feed_b(side):
        residual = jnp.concatenate([st[side, z, 0:NB] for z in range(3)], axis=0) + mix_b[side]
        out_b[side] = feed_forward(residual, wu_v[...], wd_t[...])

    late = lax.rem(la, 4) == 3
    inner = late & jnp.logical_not(end)
    first_right = far_left | end_on_left
    first = jnp.where(first_right, 1, 0)
    at_c = (jnp.where(inner, 4, jnp.where(late, 2, 1)), jnp.where(inner, 5, 3))
    at_b = (0, jnp.where(inner, 1, 4))
    at_feed = jnp.where(late & end, 1, jnp.where(inner, 3, jnp.where(end & jnp.logical_not(has_above), 5, 2)))

    def task(step, carry):
        second = (step == at_c[1]) | (step == at_b[1])
        side = jnp.where(second, 1 - first, first)
        pl.when(step == at_feed)(functools.partial(feed_b, side))
        pl.when(step == jnp.where(first_right, jnp.where(inner, 1, 2), 0))(mask)
        pl.when(step == jnp.where(late, at_c[0], 0))(rows_below)
        pl.when((step == at_c[0]) | (step == at_c[1]))(functools.partial(windows_c, side))
        pl.when((step == at_b[0]) | (step == at_b[1]))(functools.partial(windows_b, side))
        return carry

    lax.fori_loop(0, 6, task, 0)

    def put(lev, z, row, grid):
        rows = grid.shape[0] // 16
        out[(2 * z + lev + 1) % 6, row : row + rows] = grid.reshape(rows, 16, C)[:, 0:12, :].astype(BF16)

    def scatter_rows(done, row):
        for lev in range(2):
            scatter = scatter_of(lev, False)
            for z in range(3):
                put(lev, z, row, dot(scatter, done[z * 2 * NC : (z + 1) * 2 * NC].astype(BF16)))

    pairs = [(z, side) for z in range(3) for side in range(2)]
    residual = [st[1 - first, z, 0:NB] + mix_b[1 - first, z * NB : (z + 1) * NB, :] for z in range(3)]
    residual += [st[side, z, NB:BC] + mix_c[side, z * NC : (z + 1) * NC, :] for z, side in pairs]
    done = feed_forward(jnp.concatenate(residual, axis=0), wu_v[...], wd_t[...])
    out_b[1 - first] = done[0 : 3 * NB]
    scatter_rows(done[3 * NB :], 9)
    for lev in range(2):
        scatter = scatter_of(lev, True)
        for z in range(3):
            part = pl.ds(z * NB, NB)
            tokens = jnp.concatenate([out_b[0, part], out_b[1, part]], axis=0).astype(BF16)
            put(lev, z, 3, dot(scatter, tokens))

    @pl.when(has_above)
    def _():
        down(0).wait_recv()
        down(1).wait_recv()

    @pl.when(jnp.logical_not(has_above))
    def _():
        r_ret[...] = jnp.zeros_like(r_ret)

    for side in range(2):
        unpack(ret_x.at[side], r_ret.at[side], HALVED)
    residual = [st[side, z, BC : BC + NC] + ret_x[side, z * NC : (z + 1) * NC, :].astype(F32) for z, side in pairs]
    scatter_rows(feed_forward(jnp.concatenate(residual, axis=0), wu_v[...], wd_t[...]), 0)

    for copy in (along_b, along_c):
        copy(0, left).wait_send()
        copy(1, right).wait_send()
    regions.wait_send()

    @pl.when(has_above)
    def _():
        for side, (far, col) in enumerate(sides):
            pl.when(far)(corner(side, m_lat, la - 1, col).wait_send)
        up.wait_send()

    @pl.when(has_below)
    def _():
        for side, (far, col) in enumerate(sides):
            pl.when(jnp.logical_not(far))(corner(side, r_lat, la, col).wait_send)
        down(0).wait_send()
        down(1).wait_send()


def shards(n_lat, n_lon, *args):
    args = (*args[:6], args[6].T)
    args = [pltpu.with_memory_space_constraint(a, pltpu.HBM) for a in args]
    def packed(form, *lead):
        return pltpu.VMEM((*lead, form[0] + form[1], 128), BF16)

    scratch = [
        pltpu.VMEM((6, 12, 12, C), BF16),
        pltpu.VMEM((2, HEADS, 144, 144), BF16),
        pltpu.VMEM((12, 12), jnp.int32),
        pltpu.VMEM((12, 12), jnp.int32),
        pltpu.VMEM((C, 3 * C), BF16),
        pltpu.VMEM((C, C), BF16),
        pltpu.VMEM((C, C), BF16),
        pltpu.VMEM((C, C), BF16),
        pltpu.VMEM((C, C), BF16),
        pltpu.VMEM((C, FF), BF16),
        pltpu.VMEM((C, FF), BF16),
        pltpu.VMEM((FF, C), BF16),
        pltpu.VMEM((6, 12, 16, C), F32),
        pltpu.VMEM((2, 3, BC + NC, C), F32),
        pltpu.VMEM((2, 224, C), F32),
        pltpu.VMEM((2, 128, C), F32),
        pltpu.VMEM((2, 128, C), F32),
        packed(FULL, 2),
        packed(HALVED, 2),
        packed(HALVED, 2),
        packed(HALVED, 2),
        packed(FULL, 2),
        packed(HALVED, 2),
        packed(HALVED, 2),
        packed(HALVED, 2),
        packed(HALVED, 2),
        pltpu.VMEM((2, 3, 224, C), F32),
        pltpu.VMEM((2, 3, 128, C), F32),
        pltpu.VMEM((224, C), BF16),
        pltpu.VMEM((128, C), BF16),
        pltpu.VMEM((2, 128, C), BF16),
        pltpu.VMEM((128, C), BF16),
        pltpu.VMEM((2, 224, C), F32),
        pltpu.VMEM((2, 128, C), F32),
        pltpu.VMEM((2, 128, C), F32),
        pltpu.VMEM((2, 128, C), F32),
        pltpu.VMEM((2, 128, C), F32),
        pltpu.VMEM((128, C), F32),
        pltpu.VMEM((128, C), F32),
        pltpu.VMEM((2, HEADS * NB, 2 * NB), F32),
        pltpu.VMEM((2, HEADS * 2 * NC, 4 * NC), F32),
        pltpu.VMEM((16, 128), F32),
        pltpu.VMEM((2, 3 * NB, C), F32),
        pltpu.VMEM((2, 3 * NC, C), F32),
        pltpu.VMEM((128, C), F32),
        pltpu.VMEM((2, 128, C), BF16),
        pltpu.VMEM((2, 3 * NB, C), F32),
        pltpu.SemaphoreType.DMA((7,)),
        pltpu.SemaphoreType.DMA((10,)),
        pltpu.SemaphoreType.DMA((10,)),
        pltpu.SemaphoreType.REGULAR,
    ]
    return pl.pallas_call(
        functools.partial(kernel, n_lat, n_lon),
        out_shape=pltpu.VMEM((6, 12, 12, C), BF16),
        in_specs=[pl.BlockSpec(memory_space=pltpu.HBM)] * 7,
        out_specs=pl.BlockSpec(memory_space=pltpu.VMEM),
        scratch_shapes=scratch,
        compiler_params=pltpu.CompilerParams(
            collective_id=0, has_side_effects=True, vmem_limit_bytes=40 * 1024 * 1024
        ),
    )(*args)


def solution(mesh):
    placed = (
        P(None, "lat", "lon", None),
        P("lat", None, None, None),
        P("lat", "lon"),
        P(),
        P(),
        P(),
        P(),
    )
    return jax.shard_map(
        functools.partial(shards, mesh.shape["lat"], mesh.shape["lon"]),
        mesh=mesh,
        in_specs=placed,
        out_specs=P(None, "lat", "lon", None),
        check_vma=False,
    )
```
